128 devices in a mesh: seq: 16 (over y, x_hi, core), cp: 8 (over x_lo, z).
Axes of the slice: x: 4 (x_hi: 2, x_lo: 2; x = x_hi * 2 + x_lo), y: 4, z: 4, core: 2. Of those that a mesh axis runs over, the one named last changes fastest.
Arguments:
- hidden: bfloat16 [16, 1024, 1152], P('seq', 'cp'), may hold values from -6 to 6
- lengths: int32 [16], P('seq'), may hold values from 512 to 1024, as said below
- entry_gain: bfloat16 [1152], P(('seq', 'cp')), may hold values from 0.5 to 1.5
- query_weight: bfloat16 [1152, 1024], P(('seq', 'cp')), may hold values from -0.1875 to 0.1875
- key_weight: bfloat16 [1152, 256], P(('seq', 'cp')), may hold values from -0.1875 to 0.1875
- value_weight: bfloat16 [1152, 256], P(('seq', 'cp')), may hold values from -0.1875 to 0.1875
- query_gain: bfloat16 [256], P(('seq', 'cp')), may hold values from 0.5 to 1.5
- key_gain: bfloat16 [256], P(('seq', 'cp')), may hold values from 0.5 to 1.5
- output_weight: bfloat16 [1024, 1152], P(('seq', 'cp')), may hold values from -0.1875 to 0.1875
- mixer_gain: bfloat16 [1152], P(('seq', 'cp')), may hold values from 0.5 to 1.5
- feed_gain: bfloat16 [1152], P(('seq', 'cp')), may hold values from 0.5 to 1.5
- gate_weight: bfloat16 [1152, 6912], P(('seq', 'cp')), may hold values from -0.1875 to 0.1875
- up_weight: bfloat16 [1152, 6912], P(('seq', 'cp')), may hold values from -0.1875 to 0.1875
- down_weight: bfloat16 [6912, 1152], P(('seq', 'cp')), may hold values from -0.078125 to 0.078125
- closing_gain: bfloat16 [1152], P(('seq', 'cp')), may hold values from 0.5 to 1.5
- cotangent: bfloat16 [16, 1024, 1152], P('seq', 'cp'), may hold values from -6 to 6
Outputs:
- layer_output: bfloat16 [16, 1024, 1152], P('seq', 'cp')
- hidden_delta: float32 [16, 1024, 1152], P('seq', 'cp')
- entry_change: float32 [1152], P(('seq', 'cp'))
- query_delta: float32 [1152, 1024], P(('seq', 'cp'))
- key_delta: float32 [1152, 256], P(('seq', 'cp'))
- value_delta: float32 [1152, 256], P(('seq', 'cp'))
- query_change: float32 [256], P(('seq', 'cp'))
- key_change: float32 [256], P(('seq', 'cp'))
- output_delta: float32 [1024, 1152], P(('seq', 'cp'))
- mixer_change: float32 [1152], P(('seq', 'cp'))
- feed_change: float32 [1152], P(('seq', 'cp'))
- gate_delta: float32 [1152, 6912], P(('seq', 'cp'))
- upward_delta: float32 [1152, 6912], P(('seq', 'cp'))
- down_delta: float32 [6912, 1152], P(('seq', 'cp'))
- closing_change: float32 [1152], P(('seq', 'cp'))
The draws below stay inside these ranges and needn't reach their ends.
Inputs may be any that keep to these rules, and one draw needn't show every extreme that they name: `lengths`: in every draw one sequence has all 1024 slots live.
All inputs are finite; a program needn't handle non-finite values.
Results may differ from the reference program's by a relative error of at most 0.033.
Values may be sent and summed in bfloat16 or wider, within the bound.
No kernel may reach another device: no remote copies, remote signals or barrier semaphores. Data moves between devices by JAX's collectives and lax.ppermute only.
A program may use at most 384 MiB of HBM per device.

```python
import jax
import jax.numpy as jnp
from jax import lax

D = 1152
FF = 6912
HQ = 4
HD = 256
TOK_DEV = 128
LEN = 1024
GROUPS = 16
N_CP = 8


def draw_lengths(key, part):
    key = jax.random.fold_in(key, 7)
    first_key, second_key = jax.random.split(key)
    drawn = jax.random.randint(first_key, (GROUPS,), LEN // 2, LEN + 1)
    full_index = jax.random.randint(second_key, (), 0, GROUPS)
    return jnp.where(jnp.arange(GROUPS) == full_index, LEN, drawn).astype(jnp.int32)


def steps_of(rng, dims, cuts, low, top_value):
    def one(position, shards_of):
        draws = jax.random.uniform(jax.random.fold_in(jax.random.fold_in(rng, 6), position), (shards_of,), jnp.float32, low / len(cuts), top_value / len(cuts))
        return jnp.repeat(jnp.exp(draws), dims[position] // shards_of).reshape((-1,) + (1,) * (len(dims) - position - 1))

    gain = one(*cuts[0])
    for cut in cuts[1:]:
        gain = gain * one(*cut)
    return gain


def normal_values(own_key, shape, deviation, most, pieces=(), held_as=jnp.bfloat16):
    entries = deviation * jax.random.normal(own_key, shape, jnp.float32)
    if pieces:
        entries = entries * steps_of(own_key, shape, pieces, -0.22, 0.18)
    return jnp.clip(entries, -most, most).astype(held_as)


def setup_inputs(seed: int = 0) -> dict:
    keys = jax.random.split(jax.random.key(seed), 17)
    return {
        "hidden": normal_values(keys[0], (GROUPS, LEN, D), 1.0, 6.0, ((0, 16), (1, 8))),
        "lengths": draw_lengths(jax.random.fold_in(keys[16], 71), 0),
        "entry_gain": jnp.clip(1.0 + 0.1 * jax.random.normal(keys[2], (D,), jnp.float32), 0.5, 1.5).astype(jnp.bfloat16),
        "query_weight": normal_values(keys[3], (D, HQ * HD), D ** -0.5, 0.1875, ((0, 128),)),
        "key_weight": normal_values(keys[4], (D, HD), D ** -0.5, 0.1875, ((0, 128),)),
        "value_weight": normal_values(keys[5], (D, HD), D ** -0.5, 0.1875, ((0, 128),)),
        "query_gain": jnp.clip(1.0 + 0.1 * jax.random.normal(keys[6], (HD,), jnp.float32), 0.5, 1.5).astype(jnp.bfloat16),
        "key_gain": jnp.clip(1.0 + 0.1 * jax.random.normal(keys[7], (HD,), jnp.float32), 0.5, 1.5).astype(jnp.bfloat16),
        "output_weight": normal_values(keys[8], (HQ * HD, D), (HQ * HD) ** -0.5, 0.1875, ((0, 128),)),
        "mixer_gain": jnp.clip(1.0 + 0.1 * jax.random.normal(keys[9], (D,), jnp.float32), 0.5, 1.5).astype(jnp.bfloat16),
        "feed_gain": jnp.clip(1.0 + 0.1 * jax.random.normal(keys[10], (D,), jnp.float32), 0.5, 1.5).astype(jnp.bfloat16),
        "gate_weight": normal_values(keys[11], (D, FF), D ** -0.5, 0.1875, ((0, 128),)),
        "up_weight": normal_values(keys[12], (D, FF), D ** -0.5, 0.1875, ((0, 128),)),
        "down_weight": normal_values(keys[13], (FF, D), FF ** -0.5, 0.078125, ((0, 128),)),
        "closing_gain": jnp.clip(1.0 + 0.1 * jax.random.normal(keys[14], (D,), jnp.float32), 0.5, 1.5).astype(jnp.bfloat16),
        "cotangent": normal_values(keys[15], (GROUPS, LEN, D), 1.0, 6.0, ((0, 16), (1, 8))),
    }


epsilon = 1e-06

@jax.custom_vjp
def low(v):
    return lax.optimization_barrier(v.astype(jnp.bfloat16)).astype(jnp.float32)

@jax.custom_vjp
def low_back(v):
    return v

def low_keep(v):
    return (low(v), None)

def low_pass(kept, grad):
    return (grad,)

def back_keep(v):
    return (v, None)

def back_low(kept, grad):
    return (low(grad),)
low.defvjp(low_keep, low_pass)
low_back.defvjp(back_keep, back_low)

def normalize(values, scales):
    return values * lax.rsqrt(lax.optimization_barrier(jnp.mean(values * values, axis=-1, keepdims=True)) + epsilon) * scales

def folded_places(row_index, piece_rows, parts_cp):
    owner_index = row_index // (2 * piece_rows)
    inside = row_index % (2 * piece_rows)
    block_index = jnp.where(inside < piece_rows, owner_index, 2 * parts_cp - 1 - owner_index)
    return (block_index * piece_rows + inside % piece_rows).astype(jnp.int32)

def rotate(values, places):
    half_size = values.shape[-1] // 2
    frequency = 1000000.0 ** (-(jnp.arange(half_size, dtype=jnp.float32) * 2.0 / values.shape[-1]))
    angles = places.astype(jnp.float32)[:, None] * frequency[None, :]
    if values.ndim == 3:
        angles = angles[:, None, :]
    cosine = jnp.cos(angles)
    sine_part = jnp.sin(angles)
    front_half = values[..., :half_size]
    back_half = values[..., half_size:]
    return jnp.concatenate([front_half * cosine - back_half * sine_part, back_half * cosine + front_half * sine_part], axis=-1)

def query_piece(projected, scales, places, head_count):
    shaped = projected.reshape(projected.shape[0], head_count, -1)
    return rotate(normalize(shaped, scales), places) * scales.shape[0] ** (-0.5)

def key_piece(projected, scales, places):
    return rotate(normalize(projected, scales), places)

def gated(gate_out, up_out):
    return jax.nn.gelu(gate_out, approximate=True) * up_out

def group_layer(stream, live_length, params):
    entry_gain, query_weight, key_weight, value_weight, query_gain, key_gain, output_weight, mixer_gain, feed_gain, gate_weight, up_weight, down_weight, closing_gain = params
    highest = lax.Precision.HIGHEST
    count_rows = stream.shape[0]
    places = folded_places(jnp.arange(count_rows, dtype=jnp.int32), TOK_DEV // 2, N_CP)
    entry_in = low(normalize(stream, entry_gain))
    query_raw = low_back(jnp.dot(entry_in, query_weight, precision=highest))
    key_raw = low_back(jnp.dot(entry_in, key_weight, precision=highest))
    value_raw = low_back(jnp.dot(entry_in, value_weight, precision=highest))
    query_low = low(query_piece(query_raw, query_gain, places, HQ))
    key_low = low(key_piece(key_raw, key_gain, places))
    value_low = low(value_raw)
    scores = low_back(jnp.einsum('qhd,kd->hqk', query_low, key_low, precision=highest))
    allowed = (places[None, :] <= places[:, None]) & (places[None, :] < live_length)
    scores = jnp.where(allowed[None], scores, -1e+30)
    soft_low = low(jax.nn.softmax(scores, axis=-1))
    mixed = jnp.einsum('hqk,kd->qhd', soft_low, value_low, precision=highest).reshape(count_rows, HQ * HD)
    mixed = low_back(low(mixed))
    mixer_out = low_back(jnp.dot(mixed, output_weight, precision=highest))
    middle = stream + normalize(mixer_out, mixer_gain)
    feed_in = low(normalize(middle, feed_gain))
    gate_out = low_back(jnp.dot(feed_in, gate_weight, precision=highest))
    up_out = low_back(jnp.dot(feed_in, up_weight, precision=highest))
    product = low(gated(gate_out, up_out))
    down_out = low_back(jnp.dot(product, down_weight, precision=highest))
    return middle + normalize(down_out, closing_gain)

def reference(hidden, lengths, entry_gain, query_weight, key_weight, value_weight, query_gain, key_gain, output_weight, mixer_gain, feed_gain, gate_weight, up_weight, down_weight, closing_gain, cotangent):
    params = tuple((item.astype(jnp.float32) for item in (entry_gain, query_weight, key_weight, value_weight, query_gain, key_gain, output_weight, mixer_gain, feed_gain, gate_weight, up_weight, down_weight, closing_gain)))
    stream = hidden.astype(jnp.float32)

    def layer(stream, *weights):

        def single(couple):
            return group_layer(couple[0], couple[1], weights)
        return lax.map(jax.checkpoint(single), (stream, lengths))
    result, pullback = jax.vjp(layer, stream, *params)
    gradients = pullback(cotangent.astype(jnp.float32))
    return (result.astype(jnp.bfloat16), gradients[0], gradients[1], gradients[2], gradients[3], gradients[4], gradients[5], gradients[6], gradients[7], gradients[8], gradients[9], gradients[10], gradients[11], gradients[12], gradients[13])
```

```python
import jax
import jax.numpy as jnp
import numpy as np
from jax import lax
from jax.sharding import Mesh
from jax.sharding import PartitionSpec as P

NY, NXH, NC, NXL, NZ = 4, 2, 2, 2, 4
NX = NXH * NXL
AXES = ("y", "xh", "c", "xl", "z")
SEQ = ("y", "xh", "c")
CP = ("xl", "z")
XZ = ("xh", "xl", "z")
YC = ("y", "c")
D, FF, HQ, HD = 1152, 6912, 4, 256
TOK, LEN = 128, 1024
PART = FF // 8
OWN, PAD = 54, 56
WIDE = 16 * PAD
EPS = 1e-6
f32, bf16 = jnp.float32, jnp.bfloat16


def dot(a, b):
    return lax.dot_general(a, b, (((1,), (0,)), ((), ())), preferred_element_type=f32)


def dot_nt(a, b):
    return lax.dot_general(a, b, (((1,), (1,)), ((), ())), preferred_element_type=f32)


def dot_tn(a, b):
    return lax.dot_general(a, b, (((0,), (0,)), ((), ())), preferred_element_type=f32)


def split_dot_nt(a, b):
    high = a.astype(bf16)
    low = (a - high.astype(f32)).astype(bf16)
    return dot_nt(high, b) + dot_nt(low, b)


def swap(x):
    return lax.ppermute(x, "c", [(0, 1), (1, 0)])


def spread(x, axis, count):
    copies = jnp.broadcast_to(x[None], (count,) + x.shape)
    return lax.all_to_all(copies, axis, 0, 0, tiled=True)


def collect(x, axis, count):
    parts = x.reshape((count, x.shape[0] // count) + x.shape[1:])
    parts = lax.all_to_all(parts, axis, 0, 0, tiled=True)
    return jnp.sum(parts.astype(f32), axis=0)


def inverse_rms(u):
    return lax.rsqrt(jnp.mean(u * u, axis=-1, keepdims=True) + EPS)


def norm_back(dy, u, r, w):
    n = u * r
    dn = dy * w
    du = r * (dn - n * jnp.mean(dn * n, axis=-1, keepdims=True))
    return du, dy * n


def one_hot(position, width):
    return (position[:, None] == jnp.arange(width, dtype=jnp.int32)[None, :]).astype(bf16)


def owner_parts(owner):
    z = owner % NZ
    xl = (owner // NZ) % NXL
    c = (owner // (NZ * NXL)) % NC
    xh = (owner // (NZ * NXL * NC)) % NXH
    y = owner // (NZ * NXL * NC * NXH)
    return y, xh, c, xl, z


def mixer_order(rows, core):
    n = jnp.arange(128 * rows, dtype=jnp.int32)
    y, xh, c, xl, z = owner_parts(n // rows)
    half = jnp.where(c == core, 0, 1)
    return ((((half * NY + y) * NXH + xh) * NXL + xl) * NZ + z) * 9 + n % rows


def feed_order():
    n = np.arange(D)
    y, xh, c, xl, z = owner_parts(n // 9)
    return jnp.asarray((((xh * NXL + xl) * NZ + z) * 8 + y * NC + c) * 9 + n % 9, jnp.int32)


def rope_tables(cp_index):
    h = TOK // 2
    rows = np.arange(LEN)
    owner, inside = rows // TOK, rows % TOK
    block = np.where(inside < h, owner, LEN // h - 1 - owner)
    places = (block * h + inside % h).astype(np.int32)
    frequency = (1000000.0 ** (-(np.arange(HD // 2, dtype=np.float32) * 2.0 / HD))).astype(np.float32)
    angles = places.astype(np.float32)[:, None] * frequency[None, :]
    cosine, sine = np.cos(angles).astype(np.float32), np.sin(angles).astype(np.float32)

    def own(table):
        return lax.dynamic_slice_in_dim(jnp.asarray(table), cp_index * TOK, TOK, 0)

    return own(places), jnp.asarray(places), own(cosine), own(sine)


def rope(v, cosine, sine):
    a, b = v[..., : HD // 2], v[..., HD // 2 :]
    return jnp.concatenate([a * cosine - b * sine, b * cosine + a * sine], axis=-1)


def rope_back(g, cosine, sine):
    a, b = g[..., : HD // 2], g[..., HD // 2 :]
    return jnp.concatenate([a * cosine + b * sine, b * cosine - a * sine], axis=-1)


def ring_sum(x, axis, count, index):
    block = x.shape[0] // count
    total = lax.dynamic_slice_in_dim(x, index * block, block, 0).astype(f32)
    for step in (1, count - 1, 2):
        target = lax.rem(index + step, count)
        piece = lax.dynamic_slice_in_dim(x, target * block, block, 0)
        pairs = [(i, (i + step) % count) for i in range(count)]
        total = total + lax.ppermute(piece, axis, pairs).astype(f32)
    return total


def shards(
    hidden,
    lengths,
    entry_gain,
    query_weight,
    key_weight,
    value_weight,
    query_gain,
    key_gain,
    output_weight,
    mixer_gain,
    feed_gain,
    gate_weight,
    up_weight,
    down_weight,
    closing_gain,
    cotangent,
):
    core = lax.axis_index("c")
    x_index = lax.axis_index(("xh", "xl"))
    z_index = lax.axis_index("z")
    cp_index = lax.axis_index(CP)
    places_own, places_all, cosine, sine = rope_tables(cp_index)
    stream = hidden[0].astype(f32)
    upstream = cotangent[0].astype(f32)

    def columns(w):
        parts = w.reshape(9, NY, NXH, NC, PART // 2)
        return parts.transpose(1, 3, 0, 2, 4).reshape(8, 9, PART)

    to_wide = one_hot((jnp.arange(PART, dtype=jnp.int32) // OWN) * PAD + jnp.arange(PART, dtype=jnp.int32) % OWN, WIDE)
    gate_up = jnp.concatenate([columns(gate_weight), columns(up_weight)], axis=2)
    gate_up = lax.all_to_all(gate_up, YC, 0, 0, tiled=True).reshape(72, 2 * PART)
    gate_up = jnp.concatenate(
        [dot(gate_up[:, :PART], to_wide).astype(bf16), dot(gate_up[:, PART:], to_wide).astype(bf16)], axis=1
    )
    down = jnp.pad(down_weight, ((0, PAD - OWN), (0, 2 * WIDE - D)))
    feed_all = lax.all_gather(jnp.concatenate([gate_up, down], axis=0), XZ, axis=0, tiled=False)

    gains = [entry_gain, mixer_gain, feed_gain, closing_gain]
    gains += [jnp.pad(query_gain, (0, 7)), jnp.pad(key_gain, (0, 7))]
    gains = jnp.pad(jnp.stack(gains, axis=1), ((0, 0), (0, 122)))
    mixer_rows = jnp.concatenate(
        [query_weight, key_weight, value_weight, jnp.pad(output_weight, ((0, 1), (0, 0))), gains], axis=1
    )
    mixer_rows = spread(mixer_rows, XZ, 16).reshape(144, 2816)
    own_half = spread(mixer_rows, "y", NY).reshape(576, 2816)
    other_half = swap(own_half)
    project_own, project_other = own_half[:, :1536], other_half[:, :1536]
    output_own, output_other = own_half[:, 1536:2688], other_half[:, 1536:2688]

    to_mixer = one_hot(mixer_order(9, core), D)
    to_output = one_hot(mixer_order(8, core), D)
    to_feed = one_hot(feed_order(), D)
    gains = jnp.concatenate([own_half[:, 2688:], other_half[:, 2688:]], axis=0)
    gains = lax.dot_general(gains, to_mixer, (((0,), (1,)), ((), ())), preferred_element_type=f32)
    entry_scale, mixer_scale, feed_scale, closing_scale = (gains[i : i + 1] for i in range(4))
    query_scale, key_scale = gains[4:6].reshape(2, 128, 9)[:, :, :2].reshape(2, HD)

    entry_r = inverse_rms(stream)
    entry_in = dot((stream * entry_r * entry_scale).astype(bf16), to_mixer).astype(bf16)
    raw = dot(entry_in[:, :576], project_own) + dot(entry_in[:, 576:], project_other)
    query_raw = raw[:, : HQ * HD].reshape(TOK, HQ, HD).transpose(1, 0, 2)
    key_raw, value_raw = raw[:, HQ * HD : HQ * HD + HD], raw[:, HQ * HD + HD :]
    query_r, key_r = inverse_rms(query_raw), inverse_rms(key_raw)
    query_low = (rope(query_raw * query_r * query_scale, cosine, sine) * HD**-0.5).astype(bf16)
    query_low = query_low.reshape(HQ * TOK, HD)
    key_low = rope(key_raw * key_r * key_scale, cosine, sine).astype(bf16)
    couple = spread(jnp.concatenate([key_low, value_raw.astype(bf16)], axis=1), CP, 8).reshape(LEN, 2 * HD)
    key_all, value_all = couple[:, :HD], couple[:, HD:]
    allowed = (places_all[None, :] <= places_own[:, None]) & (places_all[None, :] < lengths[0])
    scores = dot_nt(query_low, key_all).reshape(HQ, TOK, LEN)
    scores = jnp.where(allowed[None], scores, -1e30)
    soft = jax.nn.softmax(scores, axis=-1).reshape(HQ * TOK, LEN)
    soft_low = soft.astype(bf16)
    mixed = dot(soft_low, value_all).astype(bf16).reshape(HQ, TOK, HD).transpose(1, 0, 2).reshape(TOK, HQ * HD)
    mixed = dot(mixed, to_output).astype(bf16)
    mixer_out = dot(mixed[:, :576], output_own) + dot(mixed[:, 576:], output_other)
    mixer_r = inverse_rms(mixer_out)
    middle = stream + mixer_out * mixer_r * mixer_scale

    gate_up = feed_all[:, :72].reshape(D, 2 * WIDE)
    down = feed_all[:, 72:, :D].reshape(WIDE, D)

    def gather_tokens(x):
        own = spread(x, "y", NY).reshape(NY * TOK, D)
        return jnp.concatenate([own, swap(own)], axis=0)

    def sum_tokens(x):
        own = x[: NY * TOK] + swap(x[NY * TOK :].astype(bf16)).astype(f32)
        return collect(own.astype(bf16), "y", NY)

    feed_r = inverse_rms(middle)
    feed_in = dot((middle * feed_r * feed_scale).astype(bf16), to_feed).astype(bf16)
    feed_in = gather_tokens(feed_in)
    gate_out = dot(feed_in, gate_up[:, :WIDE])
    up_out = dot(feed_in, gate_up[:, WIDE:])
    product = (jax.nn.gelu(gate_out, approximate=True) * up_out).astype(bf16)
    down_out = sum_tokens(dot(product, down))
    down_r = inverse_rms(down_out)
    layer_output = (middle + down_out * down_r * closing_scale).astype(bf16)

    down_grad, closing_part = norm_back(upstream, down_out, down_r, closing_scale)
    down_grad = gather_tokens(down_grad.astype(bf16))
    product_grad = dot_nt(down_grad, down)
    down_delta = dot_tn(product, down_grad).astype(bf16)
    _, gated_pull = jax.vjp(lambda g, u: jax.nn.gelu(g, approximate=True) * u, gate_out, up_out)
    gate_grad, up_grad = gated_pull(product_grad)
    gate_up_grad = jnp.concatenate([gate_grad.astype(bf16), up_grad.astype(bf16)], axis=1)
    feed_in_grad = sum_tokens(dot_nt(gate_up_grad, gate_up))
    gate_up_delta = dot_tn(feed_in, gate_up_grad).astype(bf16)

    down_share = ring_sum(down_delta, ("xh", "xl"), NX, x_index).astype(bf16)
    down_share = ring_sum(down_share, "z", NZ, z_index)[:OWN]
    gate_up_share = ring_sum(gate_up_delta, ("xh", "xl"), NX, x_index).astype(bf16)
    gate_up_share = ring_sum(gate_up_share, "z", NZ, z_index).astype(bf16)
    gate_up_share = jnp.concatenate(
        [dot_nt(gate_up_share[:, :WIDE], to_wide), dot_nt(gate_up_share[:, WIDE:], to_wide)], axis=1
    ).astype(bf16)
    gate_up_share = lax.all_to_all(gate_up_share.reshape(8, 9, 2 * PART), YC, 0, 0, tiled=True).astype(f32)

    def rows(share):
        return share.reshape(NY, NC, 9, NXH, PART // 2).transpose(2, 0, 3, 1, 4).reshape(9, FF)

    gate_delta, upward_delta = rows(gate_up_share[:, :, :PART]), rows(gate_up_share[:, :, PART:])

    feed_in_grad = split_dot_nt(feed_in_grad, to_feed)
    middle_part, feed_part = norm_back(feed_in_grad, middle, feed_r, feed_scale)
    middle_grad = upstream + middle_part
    mixer_out_grad, mixer_part = norm_back(middle_grad, mixer_out, mixer_r, mixer_scale)
    mixer_out_grad = mixer_out_grad.astype(bf16)
    mixed_grad = jnp.concatenate([dot_nt(mixer_out_grad, output_own), dot_nt(mixer_out_grad, output_other)], axis=1)
    mixed_grad = dot_nt(mixed_grad.astype(bf16), to_output).astype(bf16)
    mixed_grad = mixed_grad.reshape(TOK, HQ, HD).transpose(1, 0, 2).reshape(HQ * TOK, HD)
    value_dots = dot_nt(mixed_grad, value_all)
    score_grad = soft * (value_dots - jnp.sum(soft * value_dots, axis=-1, keepdims=True))
    score_grad = score_grad.astype(bf16)
    key_term = dot_tn(score_grad, query_low)
    value_term = dot_tn(soft_low, mixed_grad)
    couple_grad = jnp.concatenate([key_term, value_term], axis=1).astype(bf16)
    couple_grad = collect(couple_grad, CP, 8)
    key_grad, value_grad = couple_grad[:, :HD], couple_grad[:, HD:]
    query_grad = dot(score_grad, key_all).reshape(HQ, TOK, HD)
    query_grad = rope_back(query_grad * HD**-0.5, cosine, sine)
    query_raw_grad, query_part = norm_back(query_grad, query_raw, query_r, query_scale)
    key_raw_grad, key_part = norm_back(rope_back(key_grad, cosine, sine), key_raw, key_r, key_scale)
    query_raw_grad = query_raw_grad.astype(bf16).transpose(1, 0, 2).reshape(TOK, HQ * HD)
    raw_grad = jnp.concatenate([query_raw_grad, key_raw_grad.astype(bf16), value_grad.astype(bf16)], axis=1)
    entry_in_grad = jnp.concatenate([dot_nt(raw_grad, project_own), dot_nt(raw_grad, project_other)], axis=1)
    entry_in_grad = split_dot_nt(entry_in_grad, to_mixer)
    stream_part, entry_part = norm_back(entry_in_grad, stream, entry_r, entry_scale)
    hidden_delta = middle_grad + stream_part

    changes = jnp.stack([jnp.sum(t, axis=0) for t in (entry_part, mixer_part, feed_part, closing_part)], axis=0)
    head_changes = jnp.stack([jnp.sum(query_part, axis=(0, 1)), jnp.sum(key_part, axis=0)], axis=0)
    head_changes = jnp.pad(head_changes.reshape(2, 128, 2), ((0, 0), (0, 0), (0, 7))).reshape(2, D)
    changes = jnp.pad(jnp.concatenate([changes, head_changes], axis=0), ((0, 122), (0, 0))).astype(bf16)
    changes = lax.dot_general(to_mixer, changes, (((0,), (1,)), ((), ())), preferred_element_type=f32)
    mixer_delta = jnp.concatenate(
        [dot_tn(entry_in, raw_grad).astype(bf16), dot_tn(mixed, mixer_out_grad).astype(bf16), changes.astype(bf16)],
        axis=1,
    )
    mixer_delta = mixer_delta[:576].astype(f32) + swap(mixer_delta[576:]).astype(f32)
    mixer_delta = collect(mixer_delta.astype(bf16), "y", NY).astype(bf16)
    mixer_delta = collect(mixer_delta, XZ, 16)
    changes = mixer_delta[:, 2688:]

    return (
        layer_output[None],
        hidden_delta[None],
        changes[:, 0],
        mixer_delta[:, :1024],
        mixer_delta[:, 1024:1280],
        mixer_delta[:, 1280:1536],
        changes[:2, 4],
        changes[:2, 5],
        mixer_delta[:8, 1536:2688],
        changes[:, 1],
        changes[:, 2],
        gate_delta,
        upward_delta,
        down_share,
        changes[:, 3],
    )


def solution(mesh):
    chips = Mesh(mesh.devices.reshape(NY, NXH, NC, NXL, NZ), AXES)
    tokens, row, vector = P(SEQ, CP, None), P(AXES, None), P(AXES)
    return jax.shard_map(
        shards,
        mesh=chips,
        in_specs=(
            tokens, P(SEQ), vector, row, row, row, vector, vector,
            row, vector, vector, row, row, row, vector, tokens,
        ),
        out_specs=(
            tokens, tokens, vector, row, row, row, vector, vector,
            row, vector, vector, row, row, row, vector,
        ),
        check_vma=False,
    )
```

```python
import jax
import jax.numpy as jnp
import numpy as np
from jax import lax
from jax.experimental import pallas as pl
from jax.experimental.pallas import tpu as pltpu
from jax.sharding import Mesh
from jax.sharding import PartitionSpec as P

NY, NXH, NC, NXL, NZ = 4, 2, 2, 2, 4
AXES = ("y", "xh", "c", "xl", "z")
SEQ = ("y", "xh", "c")
CP = ("xl", "z")
X = ("xh", "xl")
XZ = ("xh", "xl", "z")
ZX = ("z", "xh", "xl")
YC = ("y", "c")
D, FF, HQ, HD = 1152, 6912, 4, 256
TOK, LEN = 128, 1024
PART = FF // 8
OWN, PAD = 54, 56
WIDE = 16 * PAD
EPS = 1e-6
STEPS = (0, 1, 3, 2)
f32, bf16 = jnp.float32, jnp.bfloat16


def dot(a, b):
    return lax.dot_general(a, b, (((1,), (0,)), ((), ())), preferred_element_type=f32)


def dot_nt(a, b):
    return lax.dot_general(a, b, (((1,), (1,)), ((), ())), preferred_element_type=f32)


def dot_tn(a, b):
    return lax.dot_general(a, b, (((0,), (0,)), ((), ())), preferred_element_type=f32)


def split_dot_nt(a, b):
    high = a.astype(bf16)
    low = (a - high.astype(f32)).astype(bf16)
    return dot_nt(high, b) + dot_nt(low, b)


def swap(x):
    return lax.ppermute(x, "c", [(0, 1), (1, 0)])


def fetch(x, axis, count, step):
    return lax.ppermute(x, axis, [(i, (i - step) % count) for i in range(count)])


def fetch_around(x, axis, count):
    return [x] + [fetch(x, axis, count, step) for step in STEPS[1:]]


def send_around(parts, axis, count):
    total = parts[0].astype(f32)
    for step, part in zip(STEPS[1:], parts[1:]):
        total = total + fetch(part, axis, count, -step).astype(f32)
    return total


def inverse_rms(u):
    return lax.rsqrt(jnp.mean(u * u, axis=-1, keepdims=True) + EPS)


def norm_back(dy, u, r, w):
    n = u * r
    dn = dy * w
    du = r * (dn - n * jnp.mean(dn * n, axis=-1, keepdims=True))
    return du, dy * n


def one_hot(position, width):
    return (position[:, None] == jnp.arange(width, dtype=jnp.int32)[None, :]).astype(bf16)


def owner_parts(owner):
    z = owner % NZ
    xl = (owner // NZ) % NXL
    c = (owner // (NZ * NXL)) % NC
    xh = (owner // (NZ * NXL * NC)) % NXH
    y = owner // (NZ * NXL * NC * NXH)
    return y, xh, c, xl, z


def mixer_order(rows, core, y_index):
    n = jnp.arange(128 * rows, dtype=jnp.int32)
    y, xh, c, xl, z = owner_parts(n // rows)
    step = lax.rem(y - y_index + NY, NY)
    step = jnp.where(step == 3, 2, jnp.where(step == 2, 3, step))
    block = jnp.where(c == core, 0, 1) * NY + step
    owner, inside = (xh * NXL + xl) * NZ + z, n % rows
    return block * (16 * rows) + jnp.where(inside < 8, owner * 8 + inside, 128 + owner)


def feed_order():
    n = np.arange(D)
    y, xh, c, xl, z = owner_parts(n // 9)
    owner, inside = y * NC + c, n % 9
    place = ((z * NXH + xh) * NXL + xl) * 72 + np.where(inside < 8, owner * 8 + inside, 64 + owner)
    return jnp.asarray(place, jnp.int32)


def rope_tables():
    h = TOK // 2
    rows = np.arange(LEN)
    owner, inside = rows // TOK, rows % TOK
    block = np.where(inside < h, owner, LEN // h - 1 - owner)
    places = (block * h + inside % h).astype(np.int32)
    frequency = (1000000.0 ** (-(np.arange(HD // 2, dtype=np.float32) * 2.0 / HD))).astype(np.float32)
    angles = places.astype(np.float32)[:, None] * frequency[None, :]
    return jnp.asarray(places), jnp.asarray(np.cos(angles).astype(np.float32)), jnp.asarray(np.sin(angles).astype(np.float32))


def rope(v, cosine, sine):
    a, b = v[..., : HD // 2], v[..., HD // 2 :]
    return jnp.concatenate([a * cosine - b * sine, b * cosine + a * sine], axis=-1)


def rope_back(g, cosine, sine):
    a, b = g[..., : HD // 2], g[..., HD // 2 :]
    return jnp.concatenate([a * cosine + b * sine, b * cosine - a * sine], axis=-1)


def collect(x, axis, count):
    parts = x.reshape((count, x.shape[0] // count) + x.shape[1:])
    return jnp.sum(lax.all_to_all(parts, axis, 0, 0, tiled=True).astype(f32), axis=0)


def tie(*values):
    return lax.optimization_barrier(values)


def whole(x):
    return pl.BlockSpec(x.shape, lambda i: (0, 0), pipeline_mode=pl.Buffered(1))


def turn(sources, turned):
    for k, ref in enumerate(sources):
        depth = ref.shape[0]
        turned[:, k * depth : (k + 1) * depth] = ref[...].T


def gate_up_sums(feed_in, gate_grad, up_grad):
    count, depth = len(feed_in), feed_in[0].shape[0]

    def kernel(*refs):
        feeds, gates, ups = (refs[k * count : (k + 1) * count] for k in range(3))
        out_ref, turned = refs[3 * count :]

        @pl.when(pl.program_id(0) == 0)
        def _():
            turn(feeds, turned)

        def rows(rights):
            at = pl.ds(pl.multiple_of(lax.rem(pl.program_id(0), 3) * 384, 384), 384)
            total = jnp.zeros((384, WIDE), f32)
            for k, ref in enumerate(rights):
                total += dot(turned[at, k * depth : (k + 1) * depth], ref[...])
            out_ref[...] = total.astype(bf16)

        pl.when(pl.program_id(0) < 3)(lambda: rows(gates))
        pl.when(pl.program_id(0) >= 3)(lambda: rows(ups))

    args = (*feed_in, *gate_grad, *up_grad)
    return pl.pallas_call(
        kernel,
        grid=(6,),
        in_specs=[whole(t) for t in args],
        out_specs=pl.BlockSpec((384, WIDE), lambda i: (lax.rem(i, 3), i // 3)),
        out_shape=jax.ShapeDtypeStruct((D, 2 * WIDE), bf16),
        scratch_shapes=[pltpu.VMEM((D, count * depth), bf16)],
        compiler_params=pltpu.CompilerParams(vmem_limit_bytes=40 * 2**20),
        cost_estimate=pl.CostEstimate(
            flops=4 * count * depth * D * WIDE, bytes_accessed=20 * 2**20, transcendentals=0
        ),
    )(*args)


def down_sums(product, down_grad):
    count, depth = len(product), product[0].shape[0]

    def kernel(*refs):
        out_ref, turned = refs[2 * count :]

        @pl.when(pl.program_id(0) == 0)
        def _():
            turn(refs[:count], turned)

        at = pl.multiple_of(pl.program_id(0) * 448, 448)
        total = jnp.zeros((448, D), f32)
        for k in range(count):
            total += dot(turned[pl.ds(at, 448), k * depth : (k + 1) * depth], refs[count + k][...])
        out_ref[...] = total.astype(bf16)

    args = (*product, *down_grad)
    return pl.pallas_call(
        kernel,
        grid=(2,),
        in_specs=[whole(t) for t in args],
        out_specs=pl.BlockSpec((448, D), lambda i: (i, 0)),
        out_shape=jax.ShapeDtypeStruct((WIDE, D), bf16),
        scratch_shapes=[pltpu.VMEM((WIDE, count * depth), bf16)],
        compiler_params=pltpu.CompilerParams(vmem_limit_bytes=24 * 2**20),
        cost_estimate=pl.CostEstimate(
            flops=2 * count * depth * D * WIDE, bytes_accessed=10 * 2**20, transcendentals=0
        ),
    )(*args)


def project_outer(entry_turned, query_grad, sequence_turned, key_value_grad, changes):
    tall, wide = 288, HQ * HD + 2 * HD + 128

    def kernel(entry_ref, query_ref, sequence_ref, couple_ref, changes_ref, own_ref, other_ref):
        step = pl.program_id(0)

        def store(out_ref):
            out_ref[:, : HQ * HD] = dot(entry_ref[...], query_ref[...]).astype(bf16)
            out_ref[:, HQ * HD : wide - 128] = dot(sequence_ref[...], couple_ref[...]).astype(bf16)
            out_ref[:, wide - 128 :] = changes_ref[...]

        pl.when(step < 2)(lambda: store(own_ref))
        pl.when(step >= 2)(lambda: store(other_ref))

    def rows(x):
        return pl.BlockSpec((tall, x.shape[1]), lambda i: (i, 0))

    return pl.pallas_call(
        kernel,
        grid=(4,),
        in_specs=[rows(entry_turned), whole(query_grad), rows(sequence_turned), whole(key_value_grad), rows(changes)],
        out_specs=[
            pl.BlockSpec((tall, wide), lambda i: (jnp.minimum(i, 1), 0)),
            pl.BlockSpec((tall, wide), lambda i: (jnp.maximum(i - 2, 0), 0)),
        ],
        out_shape=[jax.ShapeDtypeStruct((2 * tall, wide), bf16)] * 2,
        compiler_params=pltpu.CompilerParams(vmem_limit_bytes=24 * 2**20),
        cost_estimate=pl.CostEstimate(
            flops=2 * D * (TOK * HQ * HD + LEN * 2 * HD), bytes_accessed=9 * 2**20, transcendentals=0
        ),
    )(entry_turned, query_grad, sequence_turned, key_value_grad, changes)


def in_memory(kernel, args, outs, scratch=(), flops=0):
    vmem = pl.BlockSpec(memory_space=pltpu.VMEM)
    return pl.pallas_call(
        kernel,
        in_specs=[pl.BlockSpec(memory_space=pltpu.SMEM)] + [vmem] * (len(args) - 1),
        out_specs=[vmem] * len(outs),
        out_shape=[jax.ShapeDtypeStruct(shape, dtype) for shape, dtype in outs],
        scratch_shapes=list(scratch),
        compiler_params=pltpu.CompilerParams(vmem_limit_bytes=40 * 2**20),
        cost_estimate=pl.CostEstimate(flops=flops, bytes_accessed=2**20, transcendentals=0),
    )(*args)


def head_places():
    n = lax.broadcasted_iota(jnp.int32, (D, HD), 0)
    j = lax.broadcasted_iota(jnp.int32, (D, HD), 1)
    return (n == 9 * (j // 2) + j % 2).astype(bf16)


def project_tokens(lengths, hidden, to_mixer, pieces, other, cosine, sine):
    def kernel(_, hidden_ref, mixer_ref, *refs):
        pieces, (other_ref, cos_ref, sin_ref) = refs[:NY], refs[NY : NY + 3]
        project_ref, x_ref, in_ref, raw_ref, query_ref, couple_ref, gains_ref, scales_ref = refs[NY + 3 :]
        for k, piece in enumerate(pieces):
            project_ref[k * 144 : (k + 1) * 144, :] = piece[...]
        project_ref[576:, :] = other_ref[...]
        x = dot(hidden_ref[...], mixer_ref[...])
        x_ref[...] = x
        turned = project_ref[:, 1536:].astype(f32).T
        gains = dot_nt(turned.astype(bf16), mixer_ref[...])[:8]
        gains_ref[...] = gains
        scales = dot(gains.astype(bf16), head_places())
        scales_ref[...] = scales
        entry_in = (x * inverse_rms(x) * turned[:1]).astype(bf16)
        in_ref[...] = entry_in
        raw = dot(entry_in, project_ref[:, :1536])
        for h in range(HQ):
            at = slice(h * TOK, (h + 1) * TOK)
            head = raw[:, h * HD : (h + 1) * HD]
            raw_ref[at, :] = head
            head = rope(head * inverse_rms(head) * scales[4:5], cos_ref[...], sin_ref[...])
            query_ref[at, :] = (head * HD**-0.5).astype(bf16)
        key = raw[:, HQ * HD : HQ * HD + HD]
        key = rope(key * inverse_rms(key) * scales[5:6], cos_ref[...], sin_ref[...])
        couple_ref[:, :HD] = key.astype(bf16)
        couple_ref[:, HD:] = raw[:, HQ * HD + HD :].astype(bf16)

    outs = [
        ((D, 1664), bf16), ((TOK, D), f32), ((TOK, D), bf16), ((HQ * TOK, HD), f32),
        ((HQ * TOK, HD), bf16), ((TOK, 2 * HD), bf16), ((8, D), f32), ((8, HD), f32),
    ]
    return in_memory(kernel, (lengths, hidden, to_mixer, *pieces, other, cosine, sine), outs)


def attend(lengths, query, couple, places_own, places, to_output, pieces, other, hidden, gains, to_feed):
    def kernel(length_ref, query_ref, couple_ref, own_ref, places_ref, output_ref, *refs):
        pieces, (other_ref, hidden_ref, gains_ref, feed_ref) = refs[:NY], refs[NY : NY + 4]
        soft_ref, mixed_ref, out_ref, middle_ref, feed_in_ref, heads = refs[NY + 4 :]
        at_keys = places_ref[...]
        allowed = (at_keys <= own_ref[...]) & (at_keys < length_ref[0])
        for h in range(HQ):
            at = slice(h * TOK, (h + 1) * TOK)
            scores = jnp.where(allowed, dot_nt(query_ref[at, :], couple_ref[:, :HD]), -1e30)
            soft = jnp.exp(scores - jnp.max(scores, axis=-1, keepdims=True))
            soft = (soft / jnp.sum(soft, axis=-1, keepdims=True)).astype(bf16)
            soft_ref[at, :] = soft
            heads[:, h * HD : (h + 1) * HD] = dot(soft, couple_ref[:, HD:]).astype(bf16)
        mixed = dot(heads[...], output_ref[...]).astype(bf16)
        mixed_ref[...] = mixed
        mixer_out = dot(mixed[:, 512:], other_ref[...])
        for k, piece in enumerate(pieces):
            mixer_out += dot(mixed[:, k * 128 : (k + 1) * 128], piece[...])
        out_ref[...] = mixer_out
        middle = hidden_ref[...].astype(f32) + mixer_out * inverse_rms(mixer_out) * gains_ref[1:2, :]
        middle_ref[...] = middle
        feed_in = (middle * inverse_rms(middle) * gains_ref[2:3, :]).astype(bf16)
        feed_in_ref[...] = dot(feed_in, feed_ref[...]).astype(bf16)

    args = (lengths, query, couple, places_own, places, to_output, *pieces, other, hidden, gains, to_feed)
    outs = [((HQ * TOK, LEN), bf16), ((TOK, HQ * HD), bf16), ((TOK, D), f32), ((TOK, D), f32), ((TOK, D), bf16)]
    return in_memory(kernel, args, outs, [pltpu.VMEM((TOK, HQ * HD), bf16)])


def attend_back(
    lengths, parts, cotangent, middle, mixer_out, gains, to_feed, pieces, other, to_output, soft, couple,
    query, query_raw, key_raw, cosine, sine, cosine_own, sine_own, scales, closing_change, to_mixer,
):
    def kernel(_, *refs):
        parts, refs = refs[:NY], refs[NY:]
        cotangent_ref, middle_ref, out_ref, gains_ref, feed_ref, *pieces = refs[: 5 + NY]
        (
            other_ref, output_ref, soft_ref, couple_ref, query_ref, raw_ref, key_raw_ref, cos_ref, sin_ref,
            cos_own_ref, sin_own_ref, scales_ref, closing_ref, mixer_ref,
        ) = refs[5 + NY : 19 + NY]
        middle_grad_ref, out_grad_ref, query_grad_ref, couple_grad_ref, changes_ref, heads = refs[19 + NY :]
        feed_grad = parts[0][...]
        for part in parts[1:]:
            feed_grad += part[...].astype(f32)
        feed_grad = split_dot_nt(feed_grad, feed_ref[...])
        middle = middle_ref[...]
        middle_grad, _ = norm_back(feed_grad, middle, inverse_rms(middle), gains_ref[2:3, :])
        middle_grad += cotangent_ref[...].astype(f32)
        middle_grad_ref[...] = middle_grad
        mixer_out = out_ref[...]
        out_grad, mixer_part = norm_back(middle_grad, mixer_out, inverse_rms(mixer_out), gains_ref[1:2, :])
        out_grad = out_grad.astype(bf16)
        out_grad_ref[...] = out_grad
        for k, piece in enumerate(pieces):
            heads[:, k * 128 : (k + 1) * 128] = dot_nt(out_grad, piece[...]).astype(bf16)
        heads[:, 512:] = dot_nt(out_grad, other_ref[...]).astype(bf16)
        mixed_grad = dot_nt(heads[...], output_ref[...]).astype(bf16)
        key_grad, value_grad = jnp.zeros((LEN, HD), f32), jnp.zeros((LEN, HD), f32)
        query_change = jnp.zeros((1, HD), f32)
        for h in range(HQ):
            at = slice(h * TOK, (h + 1) * TOK)
            head = mixed_grad[:, h * HD : (h + 1) * HD]
            soft_low = soft_ref[at, :]
            soft = soft_low.astype(f32)
            value_dots = dot_nt(head, couple_ref[:, HD:])
            score_grad = soft * (value_dots - jnp.sum(soft * value_dots, axis=-1, keepdims=True))
            score_grad = score_grad.astype(bf16)
            value_grad += dot_tn(soft_low, head)
            key_grad += dot_tn(score_grad, query_ref[at, :])
            query_grad = dot(score_grad, couple_ref[:, :HD]) * HD**-0.5
            query_grad = rope_back(query_grad, cos_own_ref[...], sin_own_ref[...])
            raw = raw_ref[at, :]
            query_grad, part = norm_back(query_grad, raw, inverse_rms(raw), scales_ref[4:5, :])
            query_change += jnp.sum(part, axis=0, keepdims=True)
            query_grad_ref[:, h * HD : (h + 1) * HD] = query_grad.astype(bf16)
        raw = key_raw_ref[...]
        key_grad = rope_back(key_grad, cos_ref[...], sin_ref[...])
        key_grad, part = norm_back(key_grad, raw, inverse_rms(raw), scales_ref[5:6, :])
        couple_grad_ref[:, :HD] = key_grad.astype(bf16)
        couple_grad_ref[:, HD:] = value_grad.astype(bf16)
        key_change = jnp.sum(part, axis=0, keepdims=True)
        changes = jnp.concatenate([query_change, key_change, jnp.zeros((6, HD), f32)], axis=0).astype(bf16)
        changes = dot_nt(changes, head_places())
        mixer_change = jnp.sum(mixer_part, axis=0, keepdims=True)
        changes = jnp.concatenate([mixer_change, closing_ref[...], changes[:6], jnp.zeros((120, D), f32)], axis=0)
        changes_ref[...] = dot(changes.astype(bf16), mixer_ref[...]).T.astype(bf16)

    args = (
        lengths, *parts, cotangent, middle, mixer_out, gains, to_feed, *pieces, other, to_output, soft, couple,
        query, query_raw, key_raw, cosine, sine, cosine_own, sine_own, scales, closing_change, to_mixer,
    )
    outs = [((TOK, D), f32), ((TOK, D), bf16), ((TOK, HQ * HD), bf16), ((LEN, 2 * HD), bf16), ((D, 128), bf16)]
    return in_memory(kernel, args, outs, [pltpu.VMEM((TOK, HQ * HD), bf16)])


def shards(
    hidden,
    lengths,
    entry_gain,
    query_weight,
    key_weight,
    value_weight,
    query_gain,
    key_gain,
    output_weight,
    mixer_gain,
    feed_gain,
    gate_weight,
    up_weight,
    down_weight,
    closing_gain,
    cotangent,
):
    core = lax.axis_index("c")
    y_index = lax.axis_index("y")
    cp_index = lax.axis_index(CP)

    def fold(row):
        return jnp.pad(row, (0, 2048 - row.shape[0])).reshape(8, 256)

    gains = [entry_gain, mixer_gain, feed_gain, closing_gain]
    gains += [jnp.pad(query_gain, (0, 7)), jnp.pad(key_gain, (0, 7))]
    gains = jnp.pad(jnp.stack(gains, axis=1), ((0, 0), (0, 122)))
    project = jnp.concatenate([query_weight, key_weight, value_weight, gains], axis=1)
    mixer_rows = jnp.concatenate([project[:8], fold(project[8]), output_weight], axis=1)
    mixer_rows = jnp.broadcast_to(mixer_rows[None], (16,) + mixer_rows.shape)
    mixer_rows = lax.all_to_all(mixer_rows, XZ, 0, 0, tiled=True)
    project = jnp.concatenate(
        [mixer_rows[:, :, :1664].reshape(128, 1664), mixer_rows[:, :, 1664:1920].reshape(16, 2048)[:, :1664]], axis=0
    )

    def columns(w):
        parts = w.reshape(-1, NY, NXH, NC, PART // 2)
        return parts.transpose(1, 3, 0, 2, 4).reshape(8, -1, PART)

    unit = jnp.arange(PART, dtype=jnp.int32)
    owner = (unit // OWN % NZ) * 4 + unit // (OWN * NZ)
    to_wide = one_hot(owner * PAD + unit % OWN, WIDE)
    gate_cut, up_cut, project = tie(gate_weight, up_weight, project)
    project = fetch_around(project, "y", NY)
    main = jnp.concatenate([columns(gate_cut[:8]), columns(up_cut[:8])], axis=1)
    ninth = jnp.pad(jnp.concatenate([columns(gate_cut[8:]), columns(up_cut[8:])], axis=2), ((0, 0), (0, 0), (0, 320)))
    gate_up = jnp.concatenate([main, ninth.reshape(8, 16, 128)], axis=2)
    gate_up = lax.all_to_all(gate_up, YC, 0, 0, tiled=True)
    gate_up, *project = tie(gate_up, *project)
    ninth = gate_up[:, :, PART:].reshape(8, 2048)

    def widen(k):
        part = jnp.concatenate(
            [gate_up[:, 8 * k : 8 * k + 8, :PART].reshape(64, PART), ninth[:, PART * k : PART * (k + 1)]], axis=0
        )
        return dot(part, to_wide).astype(bf16)

    gate_up = jnp.concatenate([widen(0), widen(1)], axis=1)
    down = lax.all_gather(jnp.pad(down_weight, ((0, PAD - OWN), (0, 0))), ZX, axis=0, tiled=True)
    gate_up = lax.all_gather(gate_up, ZX, axis=0, tiled=True)

    output, *project = tie(mixer_rows[:, :, 1920:].reshape(128, D), *project)
    output = fetch_around(output, "y", NY)
    project_other = swap(jnp.concatenate(project, axis=0))

    to_mixer = one_hot(mixer_order(9, core, y_index), D)
    to_output = one_hot(mixer_order(8, core, y_index), HQ * HD)
    to_feed = one_hot(feed_order(), D)

    upstream = cotangent[0].astype(f32)
    places, cosine, sine = rope_tables()
    places_own, cosine_own, sine_own = (
        lax.dynamic_slice_in_dim(t, cp_index * TOK, TOK, 0) for t in (places, cosine, sine)
    )

    project, entry_x, entry_in, query_raw, query_low, couple, gains, scales = project_tokens(
        lengths, hidden[0], to_mixer, project, project_other, cosine_own, sine_own
    )
    entry_scale = project[:, 1536:].astype(f32).T[:1]
    project, closing_scale = project[:, :1536], gains[3:4]
    couple = lax.all_to_all(jnp.broadcast_to(couple[None], (8, TOK, 2 * HD)), CP, 0, 0, tiled=True)
    couple = couple.reshape(LEN, 2 * HD)
    sequence_x, down, couple = tie(entry_x.astype(bf16), down, couple)
    sequence_x = lax.all_gather(sequence_x, CP, axis=0, tiled=True)
    couple, *output = tie(couple, *output)
    output_other = swap(jnp.concatenate(output, axis=0))
    soft, mixed, mixer_out, middle, feed_in = attend(
        lengths, query_low, couple, places_own[:, None], places[None, :], to_output, output, output_other,
        hidden[0], gains, to_feed,
    )

    def pair(x):
        return jnp.concatenate([x, swap(x)], axis=0)

    def merge(x):
        return x[:TOK] + swap(x[TOK:].astype(bf16)).astype(f32)

    def pass_around(pieces, work):
        made, total = [], None
        for k, piece in enumerate(pieces):
            if k:
                piece, made[-1] = tie(piece, made[-1])
            made.append(work[0](k, pair(piece)))
            if k == NY - 1:
                made[-1], parts[1] = tie(made[-1], parts[1])
            part = merge(work[1](made[-1]))
            if k == 0:
                parts = [part]
            else:
                parts.append(fetch(part.astype(bf16), "y", NY, -STEPS[k]))
        total = sum(part.astype(f32) for part in parts)
        return made, total

    feed_in = fetch_around(feed_in, "y", NY)

    def forward(k, x):
        gate_out, up_out = dot(x, gate_up[:, :WIDE]), dot(x, gate_up[:, WIDE:])
        return x, gate_out, up_out, (jax.nn.gelu(gate_out, approximate=True) * up_out).astype(bf16)

    made, down_out = pass_around(feed_in, (forward, lambda t: dot(t[3], down)))
    feed_in, gate_out, up_out, product = zip(*made)
    down_r = inverse_rms(down_out)
    layer_output = (middle + down_out * down_r * closing_scale).astype(bf16)

    down_grad, closing_part = norm_back(upstream, down_out, down_r, closing_scale)
    down_grad = fetch_around(down_grad.astype(bf16), "y", NY)
    pairs = [pair(x) for x in down_grad]
    pairs[0], sequence_x = tie(pairs[0], sequence_x)
    down_delta = down_sums(product, pairs)
    pairs[-1], down_delta = tie(pairs[-1], down_delta)
    down_share = lax.psum_scatter(down_delta, "z", scatter_dimension=0, tiled=True)

    def backward(k, dy):
        _, pull = jax.vjp(lambda g, u: jax.nn.gelu(g, approximate=True) * u, gate_out[k], up_out[k])
        return tuple(t.astype(bf16) for t in pull(dot_nt(dy, down)))

    made = [backward(k, dy) for k, dy in enumerate(pairs)]
    parts = [merge(dot_nt(jnp.concatenate(t, axis=1), gate_up)) for t in made]
    feed_in_first, parts[-1] = tie(feed_in[0], parts[-1])
    sequence_x = sequence_x.astype(f32)
    sequence_in = (sequence_x * inverse_rms(sequence_x) * entry_scale).astype(bf16)
    key_raw = dot(sequence_in, project[:, HQ * HD : HQ * HD + HD])
    gate_grad, up_grad = zip(*made)
    gate_up_delta = gate_up_sums((feed_in_first, *feed_in[1:]), gate_grad, up_grad)
    parts = [parts[0]] + [fetch(part.astype(bf16), "y", NY, -step) for step, part in zip(STEPS[1:], parts[1:])]
    parts[-1], gate_up_delta = tie(parts[-1], gate_up_delta)
    gate_up_share = lax.psum_scatter(gate_up_delta, "z", scatter_dimension=0, tiled=True)
    def gain_change(weights, deltas, gain):
        total = sum(jnp.sum(w.astype(f32) * d, axis=1) for w, d in zip(weights, deltas))
        return total / gain.astype(f32)

    middle_grad, mixer_out_grad, query_raw_grad, key_value_grad, changes = attend_back(
        lengths, parts, cotangent[0], middle, mixer_out, gains, to_feed, output, output_other, to_output, soft, couple,
        query_low, query_raw, key_raw, cosine, sine, cosine_own, sine_own, scales,
        jnp.sum(closing_part, axis=0, keepdims=True), to_mixer,
    )

    project_own, project_other = project_outer(
        entry_in.T, query_raw_grad, sequence_in.T, key_value_grad, changes
    )
    output_delta = dot_tn(mixed, mixer_out_grad).astype(bf16)

    def sum_cores(own, other):
        return own.astype(f32) + swap(other).astype(f32)

    def send_chips(delta):
        block = delta.shape[0] // NY
        parts = [delta[k * block : (k + 1) * block] for k in range(NY)]
        return [parts[0]] + [fetch(p.astype(bf16), "y", NY, -step) for step, p in zip(STEPS[1:], parts[1:])]

    output_delta = send_chips(sum_cores(output_delta[:512], output_delta[512:]))
    down_share = collect(down_share, X, NXH * NXL)[:OWN]
    project_other, down_share, *output_delta = tie(project_other, down_share, *output_delta)
    project_delta = sum_cores(project_own, project_other)
    key_value_grad, project_delta = tie(key_value_grad, project_delta)
    project_delta = send_chips(project_delta)
    key_value_grad = collect(key_value_grad, CP, 8)
    key_value_grad, gate_up_share = tie(key_value_grad, gate_up_share)
    gate_up_share = collect(gate_up_share, X, NXH * NXL).astype(bf16)
    gate_up_share = gate_up_share[:, :WIDE], gate_up_share[:, WIDE:]
    gate_up_share = [dot_nt(t, to_wide).astype(bf16) for t in gate_up_share]
    main = jnp.concatenate([share[:64].reshape(8, 8, PART) for share in gate_up_share], axis=1)
    ninth = jnp.pad(jnp.concatenate([share[64:] for share in gate_up_share], axis=1), ((0, 0), (0, 320)))
    gate_up_share = jnp.concatenate([main, ninth.reshape(8, 16, 128)], axis=2)
    gate_up_share = lax.all_to_all(gate_up_share, YC, 0, 0, tiled=True).astype(f32)
    ninth = gate_up_share[:, :, PART:].reshape(8, 2048)
    gate_up_share, *project_delta = tie(gate_up_share, *project_delta)
    project_delta, output_delta = (sum(p.astype(f32) for p in parts).astype(bf16) for parts in (project_delta, output_delta))
    folded = jnp.pad(project_delta[128:], ((0, 0), (0, 2048 - 1664))).reshape(16, 8, 256)
    mixer_delta = jnp.concatenate(
        [project_delta[:128].reshape(16, 8, 1664), folded, output_delta.reshape(16, 8, D)], axis=2
    )
    mixer_delta = jnp.sum(lax.all_to_all(mixer_delta, XZ, 0, 0, tiled=True).astype(f32), axis=0)
    project_delta = jnp.concatenate([mixer_delta[:, :1664], mixer_delta[:, 1664:1920].reshape(1, 2048)[:, :1664]], axis=0)
    query_delta, key_delta, value_delta = project_delta[:, :1024], project_delta[:, 1024:1280], project_delta[:, 1280:1536]
    changes = project_delta[:, 1536:]
    entry_change = gain_change(
        (query_weight, key_weight, value_weight), (query_delta, key_delta, value_delta), entry_gain
    )

    def rows(k):
        share = jnp.concatenate(
            [gate_up_share[:, 8 * k : 8 * k + 8, :PART], ninth[:, None, PART * k : PART * (k + 1)]], axis=1
        )
        return share.reshape(NY, NC, 9, NXH, PART // 2).transpose(2, 0, 3, 1, 4).reshape(9, FF)

    gate_delta, upward_delta = rows(0), rows(1)

    feed_change = gain_change((gate_weight, up_weight), (gate_delta, upward_delta), feed_gain)

    raw_grad = jnp.concatenate([query_raw_grad, key_value_grad.astype(bf16)], axis=1)
    entry_in_grad = dot_nt(raw_grad, project)
    stream_part, _ = norm_back(entry_in_grad, entry_x, inverse_rms(entry_x), entry_scale)
    hidden_delta = middle_grad + split_dot_nt(stream_part, to_mixer)

    return (
        layer_output[None],
        hidden_delta[None],
        entry_change,
        query_delta,
        key_delta,
        value_delta,
        changes[:2, 2],
        changes[:2, 3],
        mixer_delta[:, 1920:],
        changes[:, 0],
        feed_change,
        gate_delta,
        upward_delta,
        down_share,
        changes[:, 1],
    )


def solution(mesh):
    chips = Mesh(mesh.devices.reshape(NY, NXH, NC, NXL, NZ), AXES)
    tokens, row, vector = P(SEQ, CP, None), P(AXES, None), P(AXES)
    return jax.shard_map(
        shards,
        mesh=chips,
        in_specs=(
            tokens, P(SEQ), vector, row, row, row, vector, vector,
            row, vector, vector, row, row, row, vector, tokens,
        ),
        out_specs=(
            tokens, tokens, vector, row, row, row, vector, vector,
            row, vector, vector, row, row, row, vector,
        ),
        check_vma=False,
    )
```

```python
import jax
import jax.numpy as jnp
import numpy as np
from jax import lax
from jax.experimental import pallas as pl
from jax.experimental.pallas import tpu as pltpu
from jax.sharding import Mesh
from jax.sharding import PartitionSpec as P

NY, NXH, NC, NXL, NZ = 4, 2, 2, 2, 4
AXES = ("y", "xh", "c", "xl", "z")
SEQ = ("y", "xh", "c")
CP = ("xl", "z")
X = ("xh", "xl")
XZ = ("xh", "xl", "z")
ZX = ("z", "xh", "xl")
YC = ("y", "c")
D, FF, HQ, HD = 1152, 6912, 4, 256
TOK, LEN = 128, 1024
PART = FF // 8
OWN, PAD = 54, 56
WIDE = 16 * PAD
EPS = 1e-6
STEPS = (0, 1, 3, 2)
f32, bf16 = jnp.float32, jnp.bfloat16


def dot(a, b):
    return lax.dot_general(a, b, (((1,), (0,)), ((), ())), preferred_element_type=f32)


def dot_nt(a, b):
    return lax.dot_general(a, b, (((1,), (1,)), ((), ())), preferred_element_type=f32)


def dot_tn(a, b):
    return lax.dot_general(a, b, (((0,), (0,)), ((), ())), preferred_element_type=f32)


def split_dot_nt(a, b):
    high = a.astype(bf16)
    low = (a - high.astype(f32)).astype(bf16)
    both = dot_nt(jnp.concatenate([high, low], axis=0), b)
    return both[: a.shape[0]] + both[a.shape[0] :]


def swap(x):
    return lax.ppermute(x, "c", [(0, 1), (1, 0)])


def fetch(x, axis, count, step):
    return lax.ppermute(x, axis, [(i, (i - step) % count) for i in range(count)])


def fetch_around(x, axis, count):
    return [x] + [fetch(x, axis, count, step) for step in STEPS[1:]]


def send_around(parts, axis, count):
    total = parts[0].astype(f32)
    for step, part in zip(STEPS[1:], parts[1:]):
        total = total + fetch(part, axis, count, -step).astype(f32)
    return total


def inverse_rms(u):
    return lax.rsqrt(jnp.mean(u * u, axis=-1, keepdims=True) + EPS)


def norm_back(dy, u, r, w):
    n = u * r
    dn = dy * w
    du = r * (dn - n * jnp.mean(dn * n, axis=-1, keepdims=True))
    return du, dy * n


def one_hot(position, width):
    return (position[:, None] == jnp.arange(width, dtype=jnp.int32)[None, :]).astype(bf16)


def owner_parts(owner):
    z = owner % NZ
    xl = (owner // NZ) % NXL
    c = (owner // (NZ * NXL)) % NC
    xh = (owner // (NZ * NXL * NC)) % NXH
    y = owner // (NZ * NXL * NC * NXH)
    return y, xh, c, xl, z


def mixer_order(rows, core, y_index):
    n = jnp.arange(128 * rows, dtype=jnp.int32)
    y, xh, c, xl, z = owner_parts(n // rows)
    step = lax.rem(y - y_index + NY, NY)
    step = jnp.where(step == 3, 2, jnp.where(step == 2, 3, step))
    block = jnp.where(c == core, 0, 1) * NY + step
    owner, inside = (xh * NXL + xl) * NZ + z, n % rows
    return block * (16 * rows) + jnp.where(inside < 8, owner * 8 + inside, 128 + owner)


def feed_order():
    n = np.arange(D)
    y, xh, c, xl, z = owner_parts(n // 9)
    owner, inside = y * NC + c, n % 9
    place = ((z * NXH + xh) * NXL + xl) * 72 + np.where(inside < 8, owner * 8 + inside, 64 + owner)
    return jnp.asarray(place, jnp.int32)


def rope_tables():
    h = TOK // 2
    rows = np.arange(LEN)
    owner, inside = rows // TOK, rows % TOK
    block = np.where(inside < h, owner, LEN // h - 1 - owner)
    places = (block * h + inside % h).astype(np.int32)
    frequency = (1000000.0 ** (-(np.arange(HD // 2, dtype=np.float32) * 2.0 / HD))).astype(np.float32)
    angles = places.astype(np.float32)[:, None] * frequency[None, :]
    return jnp.asarray(places), jnp.asarray(np.cos(angles).astype(np.float32)), jnp.asarray(np.sin(angles).astype(np.float32))


def rope(v, cosine, sine):
    a, b = v[..., : HD // 2], v[..., HD // 2 :]
    return jnp.concatenate([a * cosine - b * sine, b * cosine + a * sine], axis=-1)


def rope_back(g, cosine, sine):
    a, b = g[..., : HD // 2], g[..., HD // 2 :]
    return jnp.concatenate([a * cosine + b * sine, b * cosine - a * sine], axis=-1)


def ring_parts(x, axis, index):
    block = x.shape[0] // 4
    parts = [lax.dynamic_slice_in_dim(x, lax.rem(index + step, 4) * block, block, 0) for step in STEPS]
    return [parts[0]] + [fetch(part, axis, 4, -step) for step, part in zip(STEPS[1:], parts[1:])]


def collect(x, axis, count):
    parts = x.reshape((count, x.shape[0] // count) + x.shape[1:])
    return jnp.sum(lax.all_to_all(parts, axis, 0, 0, tiled=True).astype(f32), axis=0)


def tie(*values):
    return lax.optimization_barrier(values)


def whole(x):
    return pl.BlockSpec(x.shape, lambda i: (0, 0), pipeline_mode=pl.Buffered(1))


def outer_sum(left, right, tall, steps):
    depth, height = left.shape
    wide = right.shape[1] // steps
    count = height // tall

    def kernel(left_ref, right_ref, out_ref, turned):
        @pl.when(pl.program_id(0) == 0)
        def _():
            turned[...] = left_ref[...].T

        at = pl.multiple_of(lax.rem(pl.program_id(0), count) * tall, tall)
        out_ref[...] = dot(turned[pl.ds(at, tall), :], right_ref[...]).astype(bf16)

    return pl.pallas_call(
        kernel,
        grid=(count * steps,),
        in_specs=[whole(left), pl.BlockSpec((depth, wide), lambda i: (0, i // count))],
        out_specs=pl.BlockSpec((tall, wide), lambda i: (lax.rem(i, count), i // count)),
        out_shape=jax.ShapeDtypeStruct((height, right.shape[1]), bf16),
        scratch_shapes=[pltpu.VMEM((height, depth), bf16)],
        compiler_params=pltpu.CompilerParams(vmem_limit_bytes=60 * 2**20),
        cost_estimate=pl.CostEstimate(
            flops=2 * depth * height * right.shape[1], bytes_accessed=10 * 2**20, transcendentals=0
        ),
    )(left, right)


def project_outer(entry_turned, query_grad, sequence_turned, key_value_grad, changes):
    tall, wide = 288, HQ * HD + 2 * HD + 128

    def kernel(entry_ref, query_ref, sequence_ref, couple_ref, changes_ref, own_ref, other_ref):
        step = pl.program_id(0)

        def store(out_ref):
            out_ref[:, : HQ * HD] = dot(entry_ref[...], query_ref[...]).astype(bf16)
            out_ref[:, HQ * HD : wide - 128] = dot(sequence_ref[...], couple_ref[...]).astype(bf16)
            out_ref[:, wide - 128 :] = changes_ref[...]

        pl.when(step < 2)(lambda: store(own_ref))
        pl.when(step >= 2)(lambda: store(other_ref))

    def rows(x):
        return pl.BlockSpec((tall, x.shape[1]), lambda i: (i, 0))

    return pl.pallas_call(
        kernel,
        grid=(4,),
        in_specs=[rows(entry_turned), whole(query_grad), rows(sequence_turned), whole(key_value_grad), rows(changes)],
        out_specs=[
            pl.BlockSpec((tall, wide), lambda i: (jnp.minimum(i, 1), 0)),
            pl.BlockSpec((tall, wide), lambda i: (jnp.maximum(i - 2, 0), 0)),
        ],
        out_shape=[jax.ShapeDtypeStruct((2 * tall, wide), bf16)] * 2,
        compiler_params=pltpu.CompilerParams(vmem_limit_bytes=60 * 2**20),
        cost_estimate=pl.CostEstimate(flops=4 * 10**9, bytes_accessed=9 * 2**20, transcendentals=0),
    )(entry_turned, query_grad, sequence_turned, key_value_grad, changes)


class Arriving:
    def __init__(self, copy, ref):
        self.copy, self.ref, self.there = copy, ref, False
        copy.start()

    def wait(self):
        if not self.there:
            self.copy.wait()
            self.there = True

    def __getitem__(self, at):
        self.wait()
        return self.ref[at]


class Leaving:
    def __init__(self, result, ref, sent):
        self.result, self.ref, self.sent, self.copies = result, ref, sent, []

    def __getitem__(self, at):
        return self.ref[at]

    def __setitem__(self, at, value):
        self.ref[at] = value

    def leave(self, rows=None):
        result, ref = (self.result, self.ref) if rows is None else (self.result.at[rows], self.ref.at[rows])
        self.copies.append(pltpu.make_async_copy(ref, result, self.sent.at[len(self.copies)]))
        self.copies[-1].start()

    def finish(self):
        for copy in self.copies:
            copy.wait()


def in_memory(kernel, args, outs, giga, scratch=(), scalars=1):
    count, given = len(args) - scalars, len(outs)

    def body(*refs):
        sources, rest = refs[scalars : scalars + count], refs[scalars + count :]
        results, buffers, rest = rest[:given], rest[given : given + count], rest[given + count :]
        made, arrived, sent, rest = rest[:given], rest[given], rest[given + 1], rest[given + 2 :]
        operands = [
            Arriving(pltpu.make_async_copy(source, buffer, arrived.at[k]), buffer)
            for k, (source, buffer) in enumerate(zip(sources, buffers))
        ]
        results = [Leaving(result, ref, sent.at[k]) for k, (result, ref) in enumerate(zip(results, made))]
        kernel(*refs[:scalars], *operands, *results, *rest)
        for operand in operands:
            operand.wait()
        for result in results:
            if not result.copies:
                result.leave()
        for result in results:
            result.finish()

    held = [pltpu.VMEM(t.shape, t.dtype) for t in args[scalars:]] + [pltpu.VMEM(*out) for out in outs]
    size = sum(t.size * t.dtype.itemsize for t in args[scalars:])
    return pl.pallas_call(
        body,
        in_specs=[pl.BlockSpec(memory_space=pltpu.SMEM)] * scalars + [pl.BlockSpec(memory_space=pl.ANY)] * count,
        out_specs=[pl.BlockSpec(memory_space=pl.ANY)] * given,
        out_shape=[jax.ShapeDtypeStruct(shape, dtype) for shape, dtype in outs],
        scratch_shapes=held + [pltpu.SemaphoreType.DMA((count,)), pltpu.SemaphoreType.DMA((given, 4))] + list(scratch),
        compiler_params=pltpu.CompilerParams(vmem_limit_bytes=60 * 2**20),
        cost_estimate=pl.CostEstimate(flops=giga * 10**9, bytes_accessed=size, transcendentals=0),
    )(*args)


def gelu_parts(x):
    c, b = (2.0 / np.pi) ** 0.5, 0.044715
    t = jnp.tanh(c * (x + b * x * x * x))
    return 0.5 * x * (1.0 + t), 0.5 * (1.0 + t) + 0.5 * x * (1.0 - t * t) * c * (1.0 + 3.0 * b * x * x)


def feed_forward(blocks, gate_up, down):
    def kernel(*refs):
        blocks, (gate_up_ref, down_ref) = refs[: 2 * NY], refs[2 * NY : 2 * NY + 2]
        x_ref, wide_ref, product_ref, own_ref, parts_ref, others_ref = refs[2 * NY + 2 :]
        for k in range(NY):
            rows = slice(2 * k * TOK, 2 * (k + 1) * TOK)
            for j in range(2):
                x_ref[(2 * k + j) * TOK : (2 * k + j + 1) * TOK, :] = blocks[2 * k + j][...]
            gate = dot(x_ref[rows, :], gate_up_ref[:, :WIDE])
            up = dot(x_ref[rows, :], gate_up_ref[:, WIDE:])
            wide_ref[rows, :WIDE] = gate.astype(bf16)
            wide_ref[rows, WIDE:] = up.astype(bf16)
            product_ref[rows, :] = (gelu_parts(gate)[0] * up).astype(bf16)
            part = dot(product_ref[rows, :], down_ref[...])
            if k:
                parts_ref[k - 1] = part[:TOK].astype(bf16)
            else:
                own_ref[...] = part[:TOK]
            others_ref[k] = part[TOK:].astype(bf16)
            for ref in (x_ref, wide_ref, product_ref):
                ref.leave(pl.ds(2 * k * TOK, 2 * TOK))

    outs = [
        ((LEN, D), bf16), ((LEN, 2 * WIDE), bf16), ((LEN, WIDE), bf16),
        ((TOK, D), f32), ((NY - 1, TOK, D), bf16), ((NY, TOK, D), bf16),
    ]
    return in_memory(kernel, (*blocks, gate_up, down), outs, 10, scalars=0)


def feed_back(y_index, blocks, wide, gate_up, down):
    def kernel(y_ref, *refs):
        blocks, (wide_ref, gate_up_ref, down_ref) = refs[: 2 * NY], refs[2 * NY : 2 * NY + 3]
        x_ref, grad_ref, parts_ref, others_ref = refs[2 * NY + 3 :]
        for k in range(NY):
            rows = slice(2 * k * TOK, 2 * (k + 1) * TOK)
            for j in range(2):
                x_ref[(2 * k + j) * TOK : (2 * k + j + 1) * TOK, :] = blocks[2 * k + j][...]
            product_grad = dot_nt(x_ref[rows, :], down_ref[...])
            gelu, slope = gelu_parts(wide_ref[rows, :WIDE].astype(f32))
            grad_ref[rows, :WIDE] = (product_grad * wide_ref[rows, WIDE:].astype(f32) * slope).astype(bf16)
            grad_ref[rows, WIDE:] = (product_grad * gelu).astype(bf16)
            part = dot_nt(grad_ref[rows, :], gate_up_ref[...]).astype(bf16)
            chip = lax.rem(y_ref[0] + STEPS[k], NY)
            parts_ref[pl.ds(chip, 1)] = part[None, :TOK]
            others_ref[pl.ds(chip, 1)] = part[None, TOK:]
            for ref in (x_ref, grad_ref):
                ref.leave(pl.ds(2 * k * TOK, 2 * TOK))

    outs = [((LEN, D), bf16), ((LEN, 2 * WIDE), bf16), ((NY, TOK, D), bf16), ((NY, TOK, D), bf16)]
    return in_memory(kernel, (y_index, *blocks, wide, gate_up, down), outs, 13)


def sequence_keys(lengths, sequence_x, project):
    def kernel(_, x_ref, project_ref, turned_ref, key_ref):
        scale = project_ref[:, 1536:].astype(f32).T[:1]
        for k in range(8):
            at = slice(k * TOK, (k + 1) * TOK)
            x = x_ref[at, :].astype(f32)
            x = (x * inverse_rms(x) * scale).astype(bf16)
            turned_ref[:, at] = x.T
            key_ref[at, :] = dot(x, project_ref[:, HQ * HD : HQ * HD + HD])

    return in_memory(kernel, (lengths, sequence_x, project), [((D, LEN), bf16), ((LEN, HD), f32)], 2)


def head_places():
    n = lax.broadcasted_iota(jnp.int32, (D, HD), 0)
    j = lax.broadcasted_iota(jnp.int32, (D, HD), 1)
    return (n == 9 * (j // 2) + j % 2).astype(bf16)


def project_tokens(lengths, hidden, to_mixer, pieces, other, cosine, sine):
    def kernel(_, hidden_ref, mixer_ref, *refs):
        pieces, (other_ref, cos_ref, sin_ref) = refs[:NY], refs[NY : NY + 3]
        project_ref, x_ref, in_ref, raw_ref, query_ref, couple_ref, gains_ref, scales_ref = refs[NY + 3 :]
        for k, piece in enumerate(pieces):
            project_ref[k * 144 : (k + 1) * 144, :] = piece[...]
        project_ref[576:, :] = other_ref[...]
        project_ref.leave()
        x = dot(hidden_ref[...], mixer_ref[...])
        x_ref[...] = x
        turned = project_ref[:, 1536:].astype(f32).T
        gains = dot_nt(turned.astype(bf16), mixer_ref[...])[:8]
        gains_ref[...] = gains
        scales = dot(gains.astype(bf16), head_places())
        scales_ref[...] = scales
        entry_in = (x * inverse_rms(x) * turned[:1]).astype(bf16)
        in_ref[...] = entry_in.T
        in_ref.leave()
        raw = dot(entry_in, project_ref[:, :1536])
        for h in range(HQ):
            at = slice(h * TOK, (h + 1) * TOK)
            head = raw[:, h * HD : (h + 1) * HD]
            raw_ref[at, :] = head
            head = rope(head * inverse_rms(head) * scales[4:5], cos_ref[...], sin_ref[...])
            query_ref[at, :] = (head * HD**-0.5).astype(bf16)
        key = raw[:, HQ * HD : HQ * HD + HD]
        key = rope(key * inverse_rms(key) * scales[5:6], cos_ref[...], sin_ref[...])
        couple_ref[:, :HD] = key.astype(bf16)
        couple_ref[:, HD:] = raw[:, HQ * HD + HD :].astype(bf16)

    outs = [
        ((D, 1664), bf16), ((TOK, D), f32), ((D, TOK), bf16), ((HQ * TOK, HD), f32),
        ((HQ * TOK, HD), bf16), ((TOK, 2 * HD), bf16), ((8, D), f32), ((8, HD), f32),
    ]
    return in_memory(kernel, (lengths, hidden, to_mixer, *pieces, other, cosine, sine), outs, 4)


def core_lanes(even, odd, core):
    first = lax.broadcasted_iota(jnp.int32, even.shape, 1) < 64
    if core:
        return jnp.where(first, pltpu.roll(even, 64, 1), odd)
    return jnp.where(first, even, pltpu.roll(odd, 64, 1))


def split_cores(tiles, own, core):
    zero, one = core_lanes(*tiles, 0), core_lanes(*tiles, 1)
    return jnp.where((core == 0) == own, zero, one)


def attend(lengths, query, couple, places_own, places):
    def kernel(length_ref, query_ref, couple_ref, own_ref, places_ref, soft_ref, mixed_ref, heads):
        at_keys = places_ref[...]
        allowed = (at_keys <= own_ref[...]) & (at_keys < length_ref[0])
        for h in range(HQ):
            at = slice(h * TOK, (h + 1) * TOK)
            scores = jnp.where(allowed, dot_nt(query_ref[at, :], couple_ref[:, :HD]), -1e30)
            soft = jnp.exp(scores - jnp.max(scores, axis=-1, keepdims=True))
            soft = (soft / jnp.sum(soft, axis=-1, keepdims=True)).astype(bf16)
            soft_ref[at, :] = soft
            heads[:, h * HD : (h + 1) * HD] = dot(soft, couple_ref[:, HD:])
        soft_ref.leave()
        for k in range(NY):
            at = pl.multiple_of(lax.rem(length_ref[1] + STEPS[k], NY) * 256, 256)
            tiles = heads[:, pl.ds(at, 128)], heads[:, pl.ds(at + 128, 128)]
            mixed_ref[:, k * 128 : (k + 1) * 128] = split_cores(tiles, True, length_ref[2]).astype(bf16)
            mixed_ref[:, 512 + k * 128 : 640 + k * 128] = split_cores(tiles, False, length_ref[2]).astype(bf16)

    args = (lengths, query, couple, places_own, places)
    outs = [((HQ * TOK, LEN), bf16), ((TOK, HQ * HD), bf16)]
    return in_memory(kernel, args, outs, 4, [pltpu.VMEM((TOK, HQ * HD), f32)])


def mix(mixed, pieces, others, hidden, gains, to_feed):
    def kernel(mixed_ref, hidden_ref, *refs):
        pieces, (gains_ref, feed_ref, out_ref, middle_ref, feed_in_ref) = refs[: 2 * NY], refs[2 * NY :]
        mixer_out = jnp.zeros((TOK, D), f32)
        for k, piece in enumerate(pieces):
            mixer_out += dot(mixed_ref[:, k * 128 : (k + 1) * 128], piece[...])
        out_ref[...] = mixer_out
        out_ref.leave()
        middle = hidden_ref[...].astype(f32) + mixer_out * inverse_rms(mixer_out) * gains_ref[1:2, :]
        middle_ref[...] = middle
        middle_ref.leave()
        feed_in = (middle * inverse_rms(middle) * gains_ref[2:3, :]).astype(bf16)
        feed_in_ref[...] = dot(feed_in, feed_ref[...]).astype(bf16)

    args = (mixed, hidden, *pieces, *others, gains, to_feed)
    return in_memory(kernel, args, [((TOK, D), f32), ((TOK, D), f32), ((TOK, D), bf16)], 3, scalars=0)


def attend_back(
    lengths, parts, cotangent, middle, mixer_out, gains, to_feed, pieces, others, soft, couple,
    query, query_raw, key_raw, cosine, sine, cosine_own, sine_own, scales, closing_change, to_mixer, mixed,
):
    def kernel(scalars_ref, *refs):
        parts, refs = refs[0], refs[1:]
        cotangent_ref, middle_ref, out_ref, gains_ref, feed_ref, *pieces = refs[: 5 + 2 * NY]
        pieces, others = pieces[:NY], pieces[NY:]
        (
            soft_ref, couple_ref, query_ref, raw_ref, key_raw_ref, cos_ref, sin_ref,
            cos_own_ref, sin_own_ref, scales_ref, closing_ref, mixer_ref, mixed_ref,
        ) = refs[5 + 2 * NY : 18 + 2 * NY]
        middle_grad_ref, delta_ref, other_delta_ref, query_grad_ref, couple_grad_ref, changes_ref, heads = refs[18 + 2 * NY :]
        feed_grad = sum(parts[k].astype(f32) for k in range(NY))
        feed_grad = split_dot_nt(feed_grad, feed_ref[...])
        middle = middle_ref[...]
        middle_grad, _ = norm_back(feed_grad, middle, inverse_rms(middle), gains_ref[2:3, :])
        middle_grad += cotangent_ref[...].astype(f32)
        middle_grad_ref[...] = middle_grad
        middle_grad_ref.leave()
        mixer_out = out_ref[...]
        out_grad, mixer_part = norm_back(middle_grad, mixer_out, inverse_rms(mixer_out), gains_ref[1:2, :])
        out_grad = out_grad.astype(bf16)
        delta_ref[...] = dot_tn(mixed_ref[:, :512], out_grad).astype(bf16)
        other_delta_ref[...] = dot_tn(mixed_ref[:, 512:], out_grad).astype(bf16)
        delta_ref.leave()
        other_delta_ref.leave()
        for k, piece in enumerate(pieces):
            tiles = dot_nt(out_grad, piece[...]), dot_nt(out_grad, others[k][...])
            at = pl.multiple_of(lax.rem(scalars_ref[1] + STEPS[k], NY) * 256, 256)
            tiles = [jnp.where(scalars_ref[2] == 0, tiles[j], tiles[1 - j]) for j in range(2)]
            heads[:, pl.ds(at, 128)] = core_lanes(*tiles, 0)
            heads[:, pl.ds(at + 128, 128)] = core_lanes(*tiles, 1)
        mixed_grad = heads[...].astype(bf16)
        key_grad, value_grad = jnp.zeros((LEN, HD), f32), jnp.zeros((LEN, HD), f32)
        query_change = jnp.zeros((1, HD), f32)
        for h in range(HQ):
            at = slice(h * TOK, (h + 1) * TOK)
            head = mixed_grad[:, h * HD : (h + 1) * HD]
            soft_low = soft_ref[at, :]
            soft = soft_low.astype(f32)
            value_dots = dot_nt(head, couple_ref[:, HD:])
            score_grad = soft * (value_dots - jnp.sum(soft * value_dots, axis=-1, keepdims=True))
            score_grad = score_grad.astype(bf16)
            value_grad += dot_tn(soft_low, head)
            key_grad += dot_tn(score_grad, query_ref[at, :])
            query_grad = dot(score_grad, couple_ref[:, :HD]) * HD**-0.5
            query_grad = rope_back(query_grad, cos_own_ref[...], sin_own_ref[...])
            raw = raw_ref[at, :]
            query_grad, part = norm_back(query_grad, raw, inverse_rms(raw), scales_ref[4:5, :])
            query_change += jnp.sum(part, axis=0, keepdims=True)
            query_grad_ref[:, h * HD : (h + 1) * HD] = query_grad.astype(bf16)
        raw = key_raw_ref[...]
        key_grad = rope_back(key_grad, cos_ref[...], sin_ref[...])
        key_grad, part = norm_back(key_grad, raw, inverse_rms(raw), scales_ref[5:6, :])
        couple_grad_ref[:, :HD] = key_grad.astype(bf16)
        couple_grad_ref[:, HD:] = value_grad.astype(bf16)
        key_change = jnp.sum(part, axis=0, keepdims=True)
        changes = jnp.concatenate([query_change, key_change, jnp.zeros((6, HD), f32)], axis=0).astype(bf16)
        changes = dot_nt(changes, head_places())
        mixer_change = jnp.sum(mixer_part, axis=0, keepdims=True)
        changes = jnp.concatenate([mixer_change, closing_ref[...], changes[:6], jnp.zeros((120, D), f32)], axis=0)
        changes_ref[...] = dot(changes.astype(bf16), mixer_ref[...]).T.astype(bf16)

    args = (
        lengths, parts, cotangent, middle, mixer_out, gains, to_feed, *pieces, *others, soft, couple,
        query, query_raw, key_raw, cosine, sine, cosine_own, sine_own, scales, closing_change, to_mixer, mixed,
    )
    outs = [((TOK, D), f32), ((512, D), bf16), ((512, D), bf16), ((TOK, HQ * HD), bf16), ((LEN, 2 * HD), bf16), ((D, 128), bf16)]
    return in_memory(kernel, args, outs, 12, [pltpu.VMEM((TOK, HQ * HD), f32)])


def shards(
    hidden,
    lengths,
    entry_gain,
    query_weight,
    key_weight,
    value_weight,
    query_gain,
    key_gain,
    output_weight,
    mixer_gain,
    feed_gain,
    gate_weight,
    up_weight,
    down_weight,
    closing_gain,
    cotangent,
):
    core = lax.axis_index("c")
    y_index = lax.axis_index("y")
    cp_index = lax.axis_index(CP)
    x_index = lax.axis_index(X)
    xl_index = lax.axis_index("xl")
    z_index = lax.axis_index("z")

    def fold(row):
        return jnp.pad(row, (0, 2048 - row.shape[0])).reshape(8, 256)

    gains = [entry_gain, mixer_gain, feed_gain, closing_gain]
    gains += [jnp.pad(query_gain, (0, 7)), jnp.pad(key_gain, (0, 7))]
    gains = jnp.pad(jnp.stack(gains, axis=1), ((0, 0), (0, 122)))
    project = jnp.concatenate([query_weight, key_weight, value_weight, gains], axis=1)
    mixer_rows = jnp.concatenate([project[:8], fold(project[8]), output_weight], axis=1)
    mixer_rows = jnp.broadcast_to(mixer_rows[None], (16,) + mixer_rows.shape)
    mixer_rows = lax.all_to_all(mixer_rows, XZ, 0, 0, tiled=True)
    project = jnp.concatenate(
        [mixer_rows[:, :, :1664].reshape(128, 1664), mixer_rows[:, :, 1664:1920].reshape(16, 2048)[:, :1664]], axis=0
    )

    def columns(w):
        parts = w.reshape(-1, NY, NXH, NC, PART // 2)
        return parts.transpose(1, 3, 0, 2, 4).reshape(8, -1, PART)

    unit = jnp.arange(PART, dtype=jnp.int32)
    owner = (unit // OWN % NZ) * 4 + unit // (OWN * NZ)
    to_wide = one_hot(owner * PAD + unit % OWN, WIDE)
    to_mixer = one_hot(mixer_order(9, core, y_index), D)
    to_feed = one_hot(feed_order(), D)
    gate_cut, up_cut, project, to_mixer, to_feed = tie(gate_weight, up_weight, project, to_mixer, to_feed)
    project = fetch_around(project, "y", NY)
    main = jnp.concatenate([columns(gate_cut[:8]), columns(up_cut[:8])], axis=1)
    ninth = jnp.pad(jnp.concatenate([columns(gate_cut[8:]), columns(up_cut[8:])], axis=2), ((0, 0), (0, 0), (0, 320)))
    gate_up = jnp.concatenate([main, ninth.reshape(8, 16, 128)], axis=2)
    gate_up = lax.all_to_all(gate_up, YC, 0, 0, tiled=True)
    gate_up, *project = tie(gate_up, *project)
    ninth = gate_up[:, :, PART:].reshape(8, 2048)

    def widen(k):
        part = jnp.concatenate(
            [gate_up[:, 8 * k : 8 * k + 8, :PART].reshape(64, PART), ninth[:, PART * k : PART * (k + 1)]], axis=0
        )
        return dot(part, to_wide).astype(bf16)

    gate_up = jnp.concatenate([widen(0), widen(1)], axis=1)
    down = lax.all_gather(jnp.pad(down_weight, ((0, PAD - OWN), (0, 0))), ZX, axis=0, tiled=True)
    gate_up = lax.all_gather(gate_up, ZX, axis=0, tiled=True)

    output, *project = tie(mixer_rows[:, :, 1920:].reshape(128, D), *project)
    output = fetch_around(output, "y", NY)
    project_other = swap(jnp.concatenate(project, axis=0))


    upstream = cotangent[0].astype(f32)
    places, cosine, sine = rope_tables()
    places_own, cosine_own, sine_own = (
        lax.dynamic_slice_in_dim(t, cp_index * TOK, TOK, 0) for t in (places, cosine, sine)
    )

    projects, entry_x, entry_turned, query_raw, query_low, couple, gains, scales = project_tokens(
        lengths, hidden[0], to_mixer, project, project_other, cosine_own, sine_own
    )
    entry_scale = projects[:, 1536:].astype(f32).T[:1]
    project, closing_scale = projects[:, :1536], gains[3:4]
    couple = lax.all_to_all(jnp.broadcast_to(couple[None], (8, TOK, 2 * HD)), CP, 0, 0, tiled=True)
    couple = couple.reshape(LEN, 2 * HD)
    down, couple = tie(down, couple)
    scalars = jnp.stack([lengths[0], y_index, core])
    soft, mixed = attend(scalars, query_low, couple, places_own[:, None], places[None, :])
    mixed, *output = tie(mixed, *output)
    output_others = [swap(piece) for piece in output]
    mixer_out, middle, feed_in = mix(mixed, output, output_others, hidden[0], gains, to_feed)
    feed_in, sequence_x = tie(feed_in, entry_x.astype(bf16))
    sequence_x = jnp.broadcast_to(sequence_x[None], (8, TOK, D))
    sequence_x = lax.all_to_all(sequence_x, CP, 0, 0, tiled=True).reshape(LEN, D)

    def gather_tokens(own, *beside):
        pieces = fetch_around(own, "y", NY)
        pieces[1], *beside = tie(pieces[1], *beside)
        return [x for piece in pieces for x in (piece, swap(piece))], beside

    feed_x, wide, product, own_part, parts, others = feed_forward(gather_tokens(feed_in)[0], gate_up, down)
    others = swap(others).astype(f32)
    parts = [own_part + others[0]] + [(parts[k - 1] + others[k]).astype(bf16) for k in range(1, NY)]
    down_out = send_around(parts, "y", NY)
    down_r = inverse_rms(down_out)
    layer_output = (middle + down_out * down_r * closing_scale).astype(bf16)

    down_grad, closing_part = norm_back(upstream, down_out, down_r, closing_scale)
    sequence_turned, key_raw = sequence_keys(lengths, sequence_x, projects)
    blocks, (sequence_turned, key_raw) = gather_tokens(down_grad.astype(bf16), sequence_turned, key_raw)
    down_x, gate_up_grad, parts, others = feed_back(y_index[None], blocks, wide, gate_up, down)
    parts = (parts.astype(f32) + swap(others).astype(f32)).astype(bf16)
    parts, feed_x = tie(parts, feed_x)
    gate_up_delta = outer_sum(feed_x, gate_up_grad, 1152, 7)
    product, gate_up_delta = tie(product, gate_up_delta)
    down_delta = outer_sum(product, down_x, 896, 3)
    parts = lax.all_to_all(parts, "y", 0, 0, tiled=True)
    parts, gate_up_delta, down_delta = tie(parts, gate_up_delta, down_delta)
    gate_up_share = lax.psum_scatter(gate_up_delta, "z", scatter_dimension=0, tiled=True)
    down_share = lax.psum_scatter(down_delta, "z", scatter_dimension=0, tiled=True)
    def gain_change(weights, deltas, gain):
        total = sum(jnp.sum(w.astype(f32) * d, axis=1) for w, d in zip(weights, deltas))
        return total / gain.astype(f32)

    middle_grad, output_own, output_far, query_raw_grad, key_value_grad, changes = attend_back(
        scalars, parts, cotangent[0], middle, mixer_out, gains, to_feed, output, output_others, soft, couple,
        query_low, query_raw, key_raw, cosine, sine, cosine_own, sine_own, scales,
        jnp.sum(closing_part, axis=0, keepdims=True), to_mixer, mixed,
    )

    project_own, project_other = project_outer(
        entry_turned, query_raw_grad, sequence_turned, key_value_grad, changes
    )

    def sum_cores(own, other):
        return (own.astype(f32) + swap(other).astype(f32)).astype(bf16)

    def send_chips(delta):
        block = delta.shape[0] // NY
        parts = [delta[k * block : (k + 1) * block] for k in range(NY)]
        return [parts[0]] + [fetch(p.astype(bf16), "y", NY, -step) for step, p in zip(STEPS[1:], parts[1:])]

    output_delta = send_chips(sum_cores(output_own, output_far))
    project_delta = sum_cores(project_own, project_other)
    couples = key_value_grad.reshape(NXL, NZ * TOK, 2 * HD)
    kept = lax.dynamic_index_in_dim(couples, xl_index, 0, keepdims=False)
    sent = lax.dynamic_index_in_dim(couples, 1 - xl_index, 0, keepdims=False)
    sent, project_delta = tie(lax.ppermute(sent, "xl", [(0, 1), (1, 0)]), project_delta)
    project_delta = send_chips(project_delta)
    couples = (kept.astype(f32) + sent.astype(f32)).astype(bf16)
    couples, gate_up_share = tie(couples, gate_up_share)
    gate_up_share = sum(part.astype(f32) for part in ring_parts(gate_up_share, X, x_index)).astype(bf16)
    couples = ring_parts(couples, "z", z_index)
    gate_up_share, *parts = tie(gate_up_share, *project_delta, *couples)
    project_delta, key_value_grad = parts[:NY], sum(part.astype(f32) for part in parts[NY:])
    gate_up_share = gate_up_share[:, :WIDE], gate_up_share[:, WIDE:]
    gate_up_share = [dot_nt(t, to_wide).astype(bf16) for t in gate_up_share]
    main = jnp.concatenate([share[:64].reshape(8, 8, PART) for share in gate_up_share], axis=1)
    ninth = jnp.pad(jnp.concatenate([share[64:] for share in gate_up_share], axis=1), ((0, 0), (0, 320)))
    gate_up_share = jnp.concatenate([main, ninth.reshape(8, 16, 128)], axis=2)
    gate_up_share, key_value_grad = tie(gate_up_share, key_value_grad)
    gate_up_share = lax.all_to_all(gate_up_share, YC, 0, 0, tiled=True).astype(f32)
    ninth = gate_up_share[:, :, PART:].reshape(8, 2048)
    gate_up_share, down_share, *output_delta = tie(gate_up_share, down_share, *output_delta)
    project_delta, output_delta = (sum(p.astype(f32) for p in parts).astype(bf16) for parts in (project_delta, output_delta))
    folded = jnp.pad(project_delta[128:], ((0, 0), (0, 2048 - 1664))).reshape(16, 8, 256)
    mixer_delta = jnp.concatenate(
        [project_delta[:128].reshape(16, 8, 1664), folded, output_delta.reshape(16, 8, D)], axis=2
    )
    mixer_delta = lax.all_to_all(mixer_delta, XZ, 0, 0, tiled=True)
    mixer_delta, *down_parts = tie(mixer_delta, *ring_parts(down_share, X, x_index))
    down_share = sum(part.astype(f32) for part in down_parts)[:OWN]
    mixer_delta = jnp.sum(mixer_delta.astype(f32), axis=0)
    project_delta = jnp.concatenate([mixer_delta[:, :1664], mixer_delta[:, 1664:1920].reshape(1, 2048)[:, :1664]], axis=0)
    query_delta, key_delta, value_delta = project_delta[:, :1024], project_delta[:, 1024:1280], project_delta[:, 1280:1536]
    changes = project_delta[:, 1536:]
    entry_change = gain_change(
        (query_weight, key_weight, value_weight), (query_delta, key_delta, value_delta), entry_gain
    )

    def rows(k):
        share = jnp.concatenate(
            [gate_up_share[:, 8 * k : 8 * k + 8, :PART], ninth[:, None, PART * k : PART * (k + 1)]], axis=1
        )
        return share.reshape(NY, NC, 9, NXH, PART // 2).transpose(2, 0, 3, 1, 4).reshape(9, FF)

    gate_delta, upward_delta = rows(0), rows(1)

    feed_change = gain_change((gate_weight, up_weight), (gate_delta, upward_delta), feed_gain)

    raw_grad = jnp.concatenate([query_raw_grad, key_value_grad.astype(bf16)], axis=1)
    entry_in_grad = dot_nt(raw_grad, project)
    stream_part, _ = norm_back(entry_in_grad, entry_x, inverse_rms(entry_x), entry_scale)
    hidden_delta = middle_grad + split_dot_nt(stream_part, to_mixer)

    return (
        layer_output[None],
        hidden_delta[None],
        entry_change,
        query_delta,
        key_delta,
        value_delta,
        changes[:2, 2],
        changes[:2, 3],
        mixer_delta[:, 1920:],
        changes[:, 0],
        feed_change,
        gate_delta,
        upward_delta,
        down_share,
        changes[:, 1],
    )


def solution(mesh):
    chips = Mesh(mesh.devices.reshape(NY, NXH, NC, NXL, NZ), AXES)
    tokens, row, vector = P(SEQ, CP, None), P(AXES, None), P(AXES)
    return jax.shard_map(
        shards,
        mesh=chips,
        in_specs=(
            tokens, P(SEQ), vector, row, row, row, vector, vector,
            row, vector, vector, row, row, row, vector, tokens,
        ),
        out_specs=(
            tokens, tokens, vector, row, row, row, vector, vector,
            row, vector, vector, row, row, row, vector,
        ),
        check_vma=False,
    )
```

```python
import jax
import jax.numpy as jnp
import numpy as np
from jax import lax
from jax.experimental import pallas as pl
from jax.experimental.pallas import tpu as pltpu
from jax.sharding import Mesh
from jax.sharding import PartitionSpec as P

NY, NXH, NC, NXL, NZ = 4, 2, 2, 2, 4
AXES = ("y", "xh", "c", "xl", "z")
SEQ = ("y", "xh", "c")
CP = ("xl", "z")
X = ("xh", "xl")
XZ = ("xh", "xl", "z")
ZX = ("z", "xh", "xl")
YC = ("y", "c")
D, FF, HQ, HD = 1152, 6912, 4, 256
TOK, LEN = 128, 1024
PART = FF // 8
OWN, PAD = 54, 56
WIDE = 16 * PAD
EPS = 1e-6
STEPS = (0, 1, 3, 2)
f32, bf16 = jnp.float32, jnp.bfloat16


def dot(a, b):
    return lax.dot_general(a, b, (((1,), (0,)), ((), ())), preferred_element_type=f32)


def dot_nt(a, b):
    return lax.dot_general(a, b, (((1,), (1,)), ((), ())), preferred_element_type=f32)


def dot_tn(a, b):
    return lax.dot_general(a, b, (((0,), (0,)), ((), ())), preferred_element_type=f32)


def split_dot_nt(a, b):
    high = a.astype(bf16)
    low = (a - high.astype(f32)).astype(bf16)
    both = dot_nt(jnp.concatenate([high, low], axis=0), b)
    return both[: a.shape[0]] + both[a.shape[0] :]


def swap(x):
    return lax.ppermute(x, "c", [(0, 1), (1, 0)])


def fetch(x, axis, count, step):
    return lax.ppermute(x, axis, [(i, (i - step) % count) for i in range(count)])


def fetch_around(x, axis, count):
    return [x] + [fetch(x, axis, count, step) for step in STEPS[1:]]


def send_around(parts, axis, count):
    total = parts[0].astype(f32)
    for step, part in zip(STEPS[1:], parts[1:]):
        total = total + fetch(part, axis, count, -step).astype(f32)
    return total


def inverse_rms(u):
    return lax.rsqrt(jnp.mean(u * u, axis=-1, keepdims=True) + EPS)


def norm_back(dy, u, r, w):
    n = u * r
    dn = dy * w
    du = r * (dn - n * jnp.mean(dn * n, axis=-1, keepdims=True))
    return du, dy * n


def one_hot(position, width):
    return (position[:, None] == jnp.arange(width, dtype=jnp.int32)[None, :]).astype(bf16)


def owner_parts(owner):
    z = owner % NZ
    xl = (owner // NZ) % NXL
    c = (owner // (NZ * NXL)) % NC
    xh = (owner // (NZ * NXL * NC)) % NXH
    y = owner // (NZ * NXL * NC * NXH)
    return y, xh, c, xl, z


def mixer_order(rows, core, y_index):
    n = jnp.arange(128 * rows, dtype=jnp.int32)
    y, xh, c, xl, z = owner_parts(n // rows)
    step = lax.rem(y - y_index + NY, NY)
    step = jnp.where(step == 3, 2, jnp.where(step == 2, 3, step))
    block = jnp.where(c == core, 0, 1) * NY + step
    owner, inside = (xh * NXL + xl) * NZ + z, n % rows
    return block * (16 * rows) + jnp.where(inside < 8, owner * 8 + inside, 128 + owner)


def feed_order():
    n = np.arange(D)
    y, xh, c, xl, z = owner_parts(n // 9)
    owner, inside = y * NC + c, n % 9
    place = ((z * NXH + xh) * NXL + xl) * 72 + np.where(inside < 8, owner * 8 + inside, 64 + owner)
    return jnp.asarray(place, jnp.int32)


def rope_tables():
    h = TOK // 2
    rows = np.arange(LEN)
    owner, inside = rows // TOK, rows % TOK
    block = np.where(inside < h, owner, LEN // h - 1 - owner)
    places = (block * h + inside % h).astype(np.int32)
    frequency = (1000000.0 ** (-(np.arange(HD // 2, dtype=np.float32) * 2.0 / HD))).astype(np.float32)
    angles = places.astype(np.float32)[:, None] * frequency[None, :]
    return jnp.asarray(places), jnp.asarray(np.cos(angles).astype(np.float32)), jnp.asarray(np.sin(angles).astype(np.float32))


def rope(v, cosine, sine):
    a, b = v[..., : HD // 2], v[..., HD // 2 :]
    return jnp.concatenate([a * cosine - b * sine, b * cosine + a * sine], axis=-1)


def rope_back(g, cosine, sine):
    a, b = g[..., : HD // 2], g[..., HD // 2 :]
    return jnp.concatenate([a * cosine + b * sine, b * cosine - a * sine], axis=-1)


def ring_parts(x, axis, index):
    block = x.shape[0] // 4
    parts = [lax.dynamic_slice_in_dim(x, lax.rem(index + step, 4) * block, block, 0) for step in STEPS]
    return [parts[0]] + [fetch(part, axis, 4, -step) for step, part in zip(STEPS[1:], parts[1:])]


def collect(x, axis, count):
    parts = x.reshape((count, x.shape[0] // count) + x.shape[1:])
    return jnp.sum(lax.all_to_all(parts, axis, 0, 0, tiled=True).astype(f32), axis=0)


def tie(*values):
    return lax.optimization_barrier(values)


def whole(x):
    return pl.BlockSpec(x.shape, lambda i: (0, 0), pipeline_mode=pl.Buffered(1))


def outer_sum(left, right, tall, steps):
    depth, height = left.shape
    wide = right.shape[1] // steps
    count = height // tall

    def kernel(left_ref, right_ref, out_ref, turned):
        @pl.when(pl.program_id(0) == 0)
        def _():
            turned[...] = left_ref[...].T

        at = pl.multiple_of(lax.rem(pl.program_id(0), count) * tall, tall)
        out_ref[...] = dot(turned[pl.ds(at, tall), :], right_ref[...]).astype(bf16)

    return pl.pallas_call(
        kernel,
        grid=(count * steps,),
        in_specs=[whole(left), pl.BlockSpec((depth, wide), lambda i: (0, i // count))],
        out_specs=pl.BlockSpec((tall, wide), lambda i: (lax.rem(i, count), i // count)),
        out_shape=jax.ShapeDtypeStruct((height, right.shape[1]), bf16),
        scratch_shapes=[pltpu.VMEM((height, depth), bf16)],
        compiler_params=pltpu.CompilerParams(vmem_limit_bytes=60 * 2**20),
        cost_estimate=pl.CostEstimate(
            flops=2 * depth * height * right.shape[1], bytes_accessed=10 * 2**20, transcendentals=0
        ),
    )(left, right)


def project_outer(entry_turned, query_grad, sequence_turned, key_value_grad, changes):
    tall, wide = 288, HQ * HD + 2 * HD + 128

    def kernel(entry_ref, query_ref, sequence_ref, couple_ref, changes_ref, own_ref, other_ref):
        step = pl.program_id(0)

        def store(out_ref):
            out_ref[:, : HQ * HD] = dot(entry_ref[...], query_ref[...]).astype(bf16)
            out_ref[:, HQ * HD : wide - 128] = dot(sequence_ref[...], couple_ref[...]).astype(bf16)
            out_ref[:, wide - 128 :] = changes_ref[...]

        pl.when(step < 2)(lambda: store(own_ref))
        pl.when(step >= 2)(lambda: store(other_ref))

    def rows(x):
        return pl.BlockSpec((tall, x.shape[1]), lambda i: (i, 0))

    return pl.pallas_call(
        kernel,
        grid=(4,),
        in_specs=[rows(entry_turned), whole(query_grad), rows(sequence_turned), whole(key_value_grad), rows(changes)],
        out_specs=[
            pl.BlockSpec((tall, wide), lambda i: (jnp.minimum(i, 1), 0)),
            pl.BlockSpec((tall, wide), lambda i: (jnp.maximum(i - 2, 0), 0)),
        ],
        out_shape=[jax.ShapeDtypeStruct((2 * tall, wide), bf16)] * 2,
        compiler_params=pltpu.CompilerParams(vmem_limit_bytes=60 * 2**20),
        cost_estimate=pl.CostEstimate(flops=4 * 10**9, bytes_accessed=9 * 2**20, transcendentals=0),
    )(entry_turned, query_grad, sequence_turned, key_value_grad, changes)


class Arriving:
    def __init__(self, copy, ref):
        self.copy, self.ref, self.there = copy, ref, False
        copy.start()

    def wait(self):
        if not self.there:
            self.copy.wait()
            self.there = True

    def __getitem__(self, at):
        self.wait()
        return self.ref[at]


class Leaving:
    def __init__(self, result, ref, sent):
        self.result, self.ref, self.sent, self.copies = result, ref, sent, []

    def __getitem__(self, at):
        return self.ref[at]

    def __setitem__(self, at, value):
        self.ref[at] = value

    def leave(self, rows=None):
        result, ref = (self.result, self.ref) if rows is None else (self.result.at[rows], self.ref.at[rows])
        self.copies.append(pltpu.make_async_copy(ref, result, self.sent.at[len(self.copies)]))
        self.copies[-1].start()

    def finish(self):
        for copy in self.copies:
            copy.wait()


def in_memory(kernel, args, outs, giga, scratch=(), scalars=1):
    count, given = len(args) - scalars, len(outs)

    def body(*refs):
        sources, rest = refs[scalars : scalars + count], refs[scalars + count :]
        results, buffers, rest = rest[:given], rest[given : given + count], rest[given + count :]
        made, arrived, sent, rest = rest[:given], rest[given], rest[given + 1], rest[given + 2 :]
        operands = [
            Arriving(pltpu.make_async_copy(source, buffer, arrived.at[k]), buffer)
            for k, (source, buffer) in enumerate(zip(sources, buffers))
        ]
        results = [Leaving(result, ref, sent.at[k]) for k, (result, ref) in enumerate(zip(results, made))]
        kernel(*refs[:scalars], *operands, *results, *rest)
        for operand in operands:
            operand.wait()
        for result in results:
            if not result.copies:
                result.leave()
        for result in results:
            result.finish()

    held = [pltpu.VMEM(t.shape, t.dtype) for t in args[scalars:]] + [pltpu.VMEM(*out) for out in outs]
    size = sum(t.size * t.dtype.itemsize for t in args[scalars:])
    return pl.pallas_call(
        body,
        in_specs=[pl.BlockSpec(memory_space=pltpu.SMEM)] * scalars + [pl.BlockSpec(memory_space=pl.ANY)] * count,
        out_specs=[pl.BlockSpec(memory_space=pl.ANY)] * given,
        out_shape=[jax.ShapeDtypeStruct(shape, dtype) for shape, dtype in outs],
        scratch_shapes=held + [pltpu.SemaphoreType.DMA((count,)), pltpu.SemaphoreType.DMA((given, 4))] + list(scratch),
        compiler_params=pltpu.CompilerParams(vmem_limit_bytes=60 * 2**20),
        cost_estimate=pl.CostEstimate(flops=giga * 10**9, bytes_accessed=size, transcendentals=0),
    )(*args)


def gelu_parts(x):
    c, b = (2.0 / np.pi) ** 0.5, 0.044715
    t = jnp.tanh(c * (x + b * x * x * x))
    return 0.5 * x * (1.0 + t), 0.5 * (1.0 + t) + 0.5 * x * (1.0 - t * t) * c * (1.0 + 3.0 * b * x * x)


def feed_forward(blocks, gate_up, down):
    def kernel(*refs):
        blocks, (gate_up_ref, down_ref) = refs[: 2 * NY], refs[2 * NY : 2 * NY + 2]
        x_ref, wide_ref, product_ref, own_ref, parts_ref, others_ref = refs[2 * NY + 2 :]
        for k in range(NY):
            rows = slice(2 * k * TOK, 2 * (k + 1) * TOK)
            for j in range(2):
                x_ref[(2 * k + j) * TOK : (2 * k + j + 1) * TOK, :] = blocks[2 * k + j][...]
            gate = dot(x_ref[rows, :], gate_up_ref[:, :WIDE])
            up = dot(x_ref[rows, :], gate_up_ref[:, WIDE:])
            gelu, slope = gelu_parts(gate)
            wide_ref[rows, :WIDE] = (up * slope).astype(bf16)
            wide_ref[rows, WIDE:] = gelu.astype(bf16)
            product_ref[rows, :] = (gelu * up).astype(bf16)
            part = dot(product_ref[rows, :], down_ref[...])
            if k:
                parts_ref[k - 1] = part[:TOK].astype(bf16)
            else:
                own_ref[...] = part[:TOK]
            others_ref[k] = part[TOK:].astype(bf16)
            for ref in (x_ref, wide_ref, product_ref):
                ref.leave(pl.ds(2 * k * TOK, 2 * TOK))

    outs = [
        ((LEN, D), bf16), ((LEN, 2 * WIDE), bf16), ((LEN, WIDE), bf16),
        ((TOK, D), f32), ((NY - 1, TOK, D), bf16), ((NY, TOK, D), bf16),
    ]
    return in_memory(kernel, (*blocks, gate_up, down), outs, 10, scalars=0)


def feed_back(y_index, blocks, wide, gate_up, down):
    def kernel(y_ref, *refs):
        blocks, (wide_ref, gate_up_ref, down_ref) = refs[: 2 * NY], refs[2 * NY : 2 * NY + 3]
        x_ref, grad_ref, parts_ref, others_ref = refs[2 * NY + 3 :]
        for k in range(NY):
            rows = slice(2 * k * TOK, 2 * (k + 1) * TOK)
            for j in range(2):
                x_ref[(2 * k + j) * TOK : (2 * k + j + 1) * TOK, :] = blocks[2 * k + j][...]
            product_grad = dot_nt(x_ref[rows, :], down_ref[...])
            grad_ref[rows, :WIDE] = (product_grad * wide_ref[rows, :WIDE].astype(f32)).astype(bf16)
            grad_ref[rows, WIDE:] = (product_grad * wide_ref[rows, WIDE:].astype(f32)).astype(bf16)
            part = dot_nt(grad_ref[rows, :], gate_up_ref[...]).astype(bf16)
            chip = lax.rem(y_ref[0] + STEPS[k], NY)
            parts_ref[pl.ds(chip, 1)] = part[None, :TOK]
            others_ref[pl.ds(chip, 1)] = part[None, TOK:]
            for ref in (x_ref, grad_ref):
                ref.leave(pl.ds(2 * k * TOK, 2 * TOK))

    outs = [((LEN, D), bf16), ((LEN, 2 * WIDE), bf16), ((NY, TOK, D), bf16), ((NY, TOK, D), bf16)]
    return in_memory(kernel, (y_index, *blocks, wide, gate_up, down), outs, 13)


def sequence_keys(lengths, sequence_x, project):
    def kernel(_, x_ref, project_ref, turned_ref, key_ref):
        scale = project_ref[:, 1536:].astype(f32).T[:1]
        for k in range(8):
            at = slice(k * TOK, (k + 1) * TOK)
            x = x_ref[at, :].astype(f32)
            x = (x * inverse_rms(x) * scale).astype(bf16)
            turned_ref[:, at] = x.T
            key_ref[at, :] = dot(x, project_ref[:, HQ * HD : HQ * HD + HD])

    return in_memory(kernel, (lengths, sequence_x, project), [((D, LEN), bf16), ((LEN, HD), f32)], 2)


def head_places():
    n = lax.broadcasted_iota(jnp.int32, (D, HD), 0)
    j = lax.broadcasted_iota(jnp.int32, (D, HD), 1)
    return (n == 9 * (j // 2) + j % 2).astype(bf16)


def project_tokens(lengths, hidden, to_mixer, pieces, other, cosine, sine):
    def kernel(_, hidden_ref, mixer_ref, *refs):
        pieces, (other_ref, cos_ref, sin_ref) = refs[:NY], refs[NY : NY + 3]
        project_ref, x_ref, in_ref, raw_ref, query_ref, couple_ref, gains_ref, scales_ref = refs[NY + 3 :]
        for k, piece in enumerate(pieces):
            project_ref[k * 144 : (k + 1) * 144, :] = piece[...]
        project_ref[576:, :] = other_ref[...]
        project_ref.leave()
        x = dot(hidden_ref[...], mixer_ref[...])
        x_ref[...] = x
        turned = project_ref[:, 1536:].astype(f32).T
        gains = dot_nt(turned.astype(bf16), mixer_ref[...])[:8]
        gains_ref[...] = gains
        scales = dot(gains.astype(bf16), head_places())
        scales_ref[...] = scales
        entry_in = (x * inverse_rms(x) * turned[:1]).astype(bf16)
        in_ref[...] = entry_in.T
        in_ref.leave()
        raw = dot(entry_in, project_ref[:, :1536])
        for h in range(HQ):
            at = slice(h * TOK, (h + 1) * TOK)
            head = raw[:, h * HD : (h + 1) * HD]
            raw_ref[at, :] = head
            head = rope(head * inverse_rms(head) * scales[4:5], cos_ref[...], sin_ref[...])
            query_ref[at, :] = (head * HD**-0.5).astype(bf16)
        key = raw[:, HQ * HD : HQ * HD + HD]
        key = rope(key * inverse_rms(key) * scales[5:6], cos_ref[...], sin_ref[...])
        couple_ref[:, :HD] = key.astype(bf16)
        couple_ref[:, HD:] = raw[:, HQ * HD + HD :].astype(bf16)

    outs = [
        ((D, 1664), bf16), ((TOK, D), f32), ((D, TOK), bf16), ((HQ * TOK, HD), f32),
        ((HQ * TOK, HD), bf16), ((TOK, 2 * HD), bf16), ((8, D), f32), ((8, HD), f32),
    ]
    return in_memory(kernel, (lengths, hidden, to_mixer, *pieces, other, cosine, sine), outs, 4)


def core_lanes(even, odd, core):
    first = lax.broadcasted_iota(jnp.int32, even.shape, 1) < 64
    if core:
        return jnp.where(first, pltpu.roll(even, 64, 1), odd)
    return jnp.where(first, even, pltpu.roll(odd, 64, 1))


def split_cores(tiles, own, core):
    zero, one = core_lanes(*tiles, 0), core_lanes(*tiles, 1)
    return jnp.where((core == 0) == own, zero, one)


def attend(lengths, query, couple, places_own, places):
    def kernel(length_ref, query_ref, couple_ref, own_ref, places_ref, soft_ref, mixed_ref, heads):
        at_keys = places_ref[...]
        allowed = (at_keys <= own_ref[...]) & (at_keys < length_ref[0])
        for h in range(HQ):
            at = slice(h * TOK, (h + 1) * TOK)
            scores = jnp.where(allowed, dot_nt(query_ref[at, :], couple_ref[:, :HD]), -1e30)
            soft = jnp.exp(scores - jnp.max(scores, axis=-1, keepdims=True))
            soft = (soft / jnp.sum(soft, axis=-1, keepdims=True)).astype(bf16)
            soft_ref[at, :] = soft
            heads[:, h * HD : (h + 1) * HD] = dot(soft, couple_ref[:, HD:])
        soft_ref.leave()
        for k in range(NY):
            at = pl.multiple_of(lax.rem(length_ref[1] + STEPS[k], NY) * 256, 256)
            tiles = heads[:, pl.ds(at, 128)], heads[:, pl.ds(at + 128, 128)]
            mixed_ref[:, k * 128 : (k + 1) * 128] = split_cores(tiles, True, length_ref[2]).astype(bf16)
            mixed_ref[:, 512 + k * 128 : 640 + k * 128] = split_cores(tiles, False, length_ref[2]).astype(bf16)

    args = (lengths, query, couple, places_own, places)
    outs = [((HQ * TOK, LEN), bf16), ((TOK, HQ * HD), bf16)]
    return in_memory(kernel, args, outs, 4, [pltpu.VMEM((TOK, HQ * HD), f32)])


def mix(mixed, pieces, others, hidden, gains, to_feed):
    def kernel(mixed_ref, hidden_ref, *refs):
        pieces, (gains_ref, feed_ref, out_ref, middle_ref, feed_in_ref) = refs[: 2 * NY], refs[2 * NY :]
        mixer_out = jnp.zeros((TOK, D), f32)
        for k, piece in enumerate(pieces):
            mixer_out += dot(mixed_ref[:, k * 128 : (k + 1) * 128], piece[...])
        out_ref[...] = mixer_out
        out_ref.leave()
        middle = hidden_ref[...].astype(f32) + mixer_out * inverse_rms(mixer_out) * gains_ref[1:2, :]
        middle_ref[...] = middle
        middle_ref.leave()
        feed_in = (middle * inverse_rms(middle) * gains_ref[2:3, :]).astype(bf16)
        feed_in_ref[...] = dot(feed_in, feed_ref[...]).astype(bf16)

    args = (mixed, hidden, *pieces, *others, gains, to_feed)
    return in_memory(kernel, args, [((TOK, D), f32), ((TOK, D), f32), ((TOK, D), bf16)], 3, scalars=0)


def attend_back(
    lengths, parts, cotangent, middle, mixer_out, gains, to_feed, pieces, others, soft, couple,
    query, query_raw, key_raw, cosine, sine, cosine_own, sine_own, scales, closing_change, to_mixer, mixed,
):
    def kernel(scalars_ref, *refs):
        parts, refs = refs[0], refs[1:]
        cotangent_ref, middle_ref, out_ref, gains_ref, feed_ref, *pieces = refs[: 5 + 2 * NY]
        pieces, others = pieces[:NY], pieces[NY:]
        (
            soft_ref, couple_ref, query_ref, raw_ref, key_raw_ref, cos_ref, sin_ref,
            cos_own_ref, sin_own_ref, scales_ref, closing_ref, mixer_ref, mixed_ref,
        ) = refs[5 + 2 * NY : 18 + 2 * NY]
        middle_grad_ref, delta_ref, other_delta_ref, query_grad_ref, couple_grad_ref, changes_ref, heads = refs[18 + 2 * NY :]
        feed_grad = sum(parts[k].astype(f32) for k in range(NY))
        feed_grad = split_dot_nt(feed_grad, feed_ref[...])
        middle = middle_ref[...]
        middle_grad, _ = norm_back(feed_grad, middle, inverse_rms(middle), gains_ref[2:3, :])
        middle_grad += cotangent_ref[...].astype(f32)
        middle_grad_ref[...] = middle_grad
        middle_grad_ref.leave()
        mixer_out = out_ref[...]
        out_grad, mixer_part = norm_back(middle_grad, mixer_out, inverse_rms(mixer_out), gains_ref[1:2, :])
        out_grad = out_grad.astype(bf16)
        delta_ref[...] = dot_tn(mixed_ref[:, :512], out_grad).astype(bf16)
        other_delta_ref[...] = dot_tn(mixed_ref[:, 512:], out_grad).astype(bf16)
        delta_ref.leave()
        other_delta_ref.leave()
        for k, piece in enumerate(pieces):
            tiles = dot_nt(out_grad, piece[...]), dot_nt(out_grad, others[k][...])
            at = pl.multiple_of(lax.rem(scalars_ref[1] + STEPS[k], NY) * 256, 256)
            tiles = [jnp.where(scalars_ref[2] == 0, tiles[j], tiles[1 - j]) for j in range(2)]
            heads[:, pl.ds(at, 128)] = core_lanes(*tiles, 0)
            heads[:, pl.ds(at + 128, 128)] = core_lanes(*tiles, 1)
        mixed_grad = heads[...].astype(bf16)
        key_grad, value_grad = jnp.zeros((LEN, HD), f32), jnp.zeros((LEN, HD), f32)
        query_change = jnp.zeros((1, HD), f32)
        for h in range(HQ):
            at = slice(h * TOK, (h + 1) * TOK)
            head = mixed_grad[:, h * HD : (h + 1) * HD]
            soft_low = soft_ref[at, :]
            soft = soft_low.astype(f32)
            value_dots = dot_nt(head, couple_ref[:, HD:])
            score_grad = soft * (value_dots - jnp.sum(soft * value_dots, axis=-1, keepdims=True))
            score_grad = score_grad.astype(bf16)
            value_grad += dot_tn(soft_low, head)
            key_grad += dot_tn(score_grad, query_ref[at, :])
            query_grad = dot(score_grad, couple_ref[:, :HD]) * HD**-0.5
            query_grad = rope_back(query_grad, cos_own_ref[...], sin_own_ref[...])
            raw = raw_ref[at, :]
            query_grad, part = norm_back(query_grad, raw, inverse_rms(raw), scales_ref[4:5, :])
            query_change += jnp.sum(part, axis=0, keepdims=True)
            query_grad_ref[:, h * HD : (h + 1) * HD] = query_grad.astype(bf16)
        raw = key_raw_ref[...]
        key_grad = rope_back(key_grad, cos_ref[...], sin_ref[...])
        key_grad, part = norm_back(key_grad, raw, inverse_rms(raw), scales_ref[5:6, :])
        couple_grad_ref[:, :HD] = key_grad.astype(bf16)
        couple_grad_ref[:, HD:] = value_grad.astype(bf16)
        key_change = jnp.sum(part, axis=0, keepdims=True)
        changes = jnp.concatenate([query_change, key_change, jnp.zeros((6, HD), f32)], axis=0).astype(bf16)
        changes = dot_nt(changes, head_places())
        mixer_change = jnp.sum(mixer_part, axis=0, keepdims=True)
        changes = jnp.concatenate([mixer_change, closing_ref[...], changes[:6], jnp.zeros((120, D), f32)], axis=0)
        changes_ref[...] = dot(changes.astype(bf16), mixer_ref[...]).T.astype(bf16)

    args = (
        lengths, parts, cotangent, middle, mixer_out, gains, to_feed, *pieces, *others, soft, couple,
        query, query_raw, key_raw, cosine, sine, cosine_own, sine_own, scales, closing_change, to_mixer, mixed,
    )
    outs = [((TOK, D), f32), ((512, D), bf16), ((512, D), bf16), ((TOK, HQ * HD), bf16), ((LEN, 2 * HD), bf16), ((D, 128), bf16)]
    return in_memory(kernel, args, outs, 12, [pltpu.VMEM((TOK, HQ * HD), f32)])


def shards(
    hidden,
    lengths,
    entry_gain,
    query_weight,
    key_weight,
    value_weight,
    query_gain,
    key_gain,
    output_weight,
    mixer_gain,
    feed_gain,
    gate_weight,
    up_weight,
    down_weight,
    closing_gain,
    cotangent,
):
    core = lax.axis_index("c")
    y_index = lax.axis_index("y")
    cp_index = lax.axis_index(CP)
    x_index = lax.axis_index(X)
    xl_index = lax.axis_index("xl")
    z_index = lax.axis_index("z")

    def fold(row):
        return jnp.pad(row, (0, 2048 - row.shape[0])).reshape(8, 256)

    gains = [entry_gain, mixer_gain, feed_gain, closing_gain]
    gains += [jnp.pad(query_gain, (0, 7)), jnp.pad(key_gain, (0, 7))]
    gains = jnp.pad(jnp.stack(gains, axis=1), ((0, 0), (0, 122)))
    project = jnp.concatenate([query_weight, key_weight, value_weight, gains], axis=1)
    mixer_rows = jnp.concatenate([project[:8], fold(project[8]), output_weight], axis=1)
    mixer_rows = jnp.broadcast_to(mixer_rows[None], (16,) + mixer_rows.shape)
    mixer_rows = lax.all_to_all(mixer_rows, XZ, 0, 0, tiled=True)
    project = jnp.concatenate(
        [mixer_rows[:, :, :1664].reshape(128, 1664), mixer_rows[:, :, 1664:1920].reshape(16, 2048)[:, :1664]], axis=0
    )

    def columns(w):
        parts = w.reshape(-1, NY, NXH, NC, PART // 2)
        return parts.transpose(1, 3, 0, 2, 4).reshape(8, -1, PART)

    unit = jnp.arange(PART, dtype=jnp.int32)
    owner = (unit // OWN % NZ) * 4 + unit // (OWN * NZ)
    to_wide = one_hot(owner * PAD + unit % OWN, WIDE)
    to_mixer = one_hot(mixer_order(9, core, y_index), D)
    to_feed = one_hot(feed_order(), D)
    gate_cut, up_cut, project, to_mixer, to_feed = tie(gate_weight, up_weight, project, to_mixer, to_feed)
    project = fetch_around(project, "y", NY)
    main = jnp.concatenate([columns(gate_cut[:8]), columns(up_cut[:8])], axis=1)
    ninth = jnp.pad(jnp.concatenate([columns(gate_cut[8:]), columns(up_cut[8:])], axis=2), ((0, 0), (0, 0), (0, 320)))
    gate_up = jnp.concatenate([main, ninth.reshape(8, 16, 128)], axis=2)
    gate_up = lax.all_to_all(gate_up, YC, 0, 0, tiled=True)
    gate_up, *project = tie(gate_up, *project)
    ninth = gate_up[:, :, PART:].reshape(8, 2048)

    def widen(k):
        part = jnp.concatenate(
            [gate_up[:, 8 * k : 8 * k + 8, :PART].reshape(64, PART), ninth[:, PART * k : PART * (k + 1)]], axis=0
        )
        return dot(part, to_wide).astype(bf16)

    gate_up = jnp.concatenate([widen(0), widen(1)], axis=1)
    down = lax.all_gather(jnp.pad(down_weight, ((0, PAD - OWN), (0, 0))), ZX, axis=0, tiled=True)
    gate_up = lax.all_gather(gate_up, ZX, axis=0, tiled=True)

    output, *project = tie(mixer_rows[:, :, 1920:].reshape(128, D), *project)
    output = fetch_around(output, "y", NY)
    project_other = swap(jnp.concatenate(project, axis=0))


    upstream = cotangent[0].astype(f32)
    places, cosine, sine = rope_tables()
    places_own, cosine_own, sine_own = (
        lax.dynamic_slice_in_dim(t, cp_index * TOK, TOK, 0) for t in (places, cosine, sine)
    )

    projects, entry_x, entry_turned, query_raw, query_low, couple, gains, scales = project_tokens(
        lengths, hidden[0], to_mixer, project, project_other, cosine_own, sine_own
    )
    entry_scale = projects[:, 1536:].astype(f32).T[:1]
    project, closing_scale = projects[:, :1536], gains[3:4]
    couple = lax.all_to_all(jnp.broadcast_to(couple[None], (8, TOK, 2 * HD)), CP, 0, 0, tiled=True)
    couple = couple.reshape(LEN, 2 * HD)
    down, couple = tie(down, couple)
    scalars = jnp.stack([lengths[0], y_index, core])
    soft, mixed = attend(scalars, query_low, couple, places_own[:, None], places[None, :])
    mixed, *output = tie(mixed, *output)
    output_others = [swap(piece) for piece in output]
    mixer_out, middle, feed_in = mix(mixed, output, output_others, hidden[0], gains, to_feed)
    feed_in, sequence_x = tie(feed_in, entry_x.astype(bf16))
    sequence_x = jnp.broadcast_to(sequence_x[None], (8, TOK, D))
    sequence_x = lax.all_to_all(sequence_x, CP, 0, 0, tiled=True).reshape(LEN, D)

    def gather_tokens(own, *beside):
        pieces = fetch_around(own, "y", NY)
        pieces[1], *beside = tie(pieces[1], *beside)
        return [x for piece in pieces for x in (piece, swap(piece))], beside

    feed_x, wide, product, own_part, parts, others = feed_forward(gather_tokens(feed_in)[0], gate_up, down)
    others = swap(others).astype(f32)
    parts = [own_part + others[0]] + [(parts[k - 1] + others[k]).astype(bf16) for k in range(1, NY)]
    down_out = send_around(parts, "y", NY)
    down_r = inverse_rms(down_out)
    layer_output = (middle + down_out * down_r * closing_scale).astype(bf16)

    down_grad, closing_part = norm_back(upstream, down_out, down_r, closing_scale)
    sequence_turned, key_raw = sequence_keys(lengths, sequence_x, projects)
    blocks, (sequence_turned, key_raw) = gather_tokens(down_grad.astype(bf16), sequence_turned, key_raw)
    down_x, gate_up_grad, parts, others = feed_back(y_index[None], blocks, wide, gate_up, down)
    parts = (parts.astype(f32) + swap(others).astype(f32)).astype(bf16)
    parts, feed_x = tie(parts, feed_x)
    gate_up_delta = outer_sum(feed_x, gate_up_grad, 1152, 7)
    parts = lax.all_to_all(parts, "y", 0, 0, tiled=True)
    parts, gate_up_delta = tie(parts, gate_up_delta)
    gate_up_share = lax.psum_scatter(gate_up_delta, "z", scatter_dimension=0, tiled=True)
    def gain_change(weights, deltas, gain):
        total = sum(jnp.sum(w.astype(f32) * d, axis=1) for w, d in zip(weights, deltas))
        return total / gain.astype(f32)

    middle_grad, output_own, output_far, query_raw_grad, key_value_grad, changes = attend_back(
        scalars, parts, cotangent[0], middle, mixer_out, gains, to_feed, output, output_others, soft, couple,
        query_low, query_raw, key_raw, cosine, sine, cosine_own, sine_own, scales,
        jnp.sum(closing_part, axis=0, keepdims=True), to_mixer, mixed,
    )

    project_own, project_other = project_outer(
        entry_turned, query_raw_grad, sequence_turned, key_value_grad, changes
    )

    def sum_cores(own, other):
        return (own.astype(f32) + swap(other).astype(f32)).astype(bf16)

    def send_chips(delta):
        block = delta.shape[0] // NY
        parts = [delta[k * block : (k + 1) * block] for k in range(NY)]
        return [parts[0]] + [fetch(p.astype(bf16), "y", NY, -step) for step, p in zip(STEPS[1:], parts[1:])]

    output_delta = send_chips(sum_cores(output_own, output_far))
    project_delta = sum_cores(project_own, project_other)
    couples = key_value_grad.reshape(NXL, NZ * TOK, 2 * HD)
    kept = lax.dynamic_index_in_dim(couples, xl_index, 0, keepdims=False)
    sent = lax.dynamic_index_in_dim(couples, 1 - xl_index, 0, keepdims=False)
    product, project_delta = tie(product, project_delta)
    project_delta = send_chips(project_delta)
    down_delta = outer_sum(product, down_x, 896, 3)
    down_share = lax.psum_scatter(down_delta, "z", scatter_dimension=0, tiled=True)
    sent = lax.ppermute(sent, "xl", [(0, 1), (1, 0)])
    project_delta[1], sent, gate_up_share = tie(project_delta[1], sent, gate_up_share)
    couples = (kept.astype(f32) + sent.astype(f32)).astype(bf16)
    gate_up_share = sum(part.astype(f32) for part in ring_parts(gate_up_share, X, x_index)).astype(bf16)
    couples = ring_parts(couples, "z", z_index)
    gate_up_share, *project_delta = tie(gate_up_share, *project_delta)
    key_value_grad = sum(part.astype(f32) for part in couples)
    gate_up_share = gate_up_share[:, :WIDE], gate_up_share[:, WIDE:]
    gate_up_share = [dot_nt(t, to_wide).astype(bf16) for t in gate_up_share]
    main = jnp.concatenate([share[:64].reshape(8, 8, PART) for share in gate_up_share], axis=1)
    ninth = jnp.pad(jnp.concatenate([share[64:] for share in gate_up_share], axis=1), ((0, 0), (0, 320)))
    gate_up_share = jnp.concatenate([main, ninth.reshape(8, 16, 128)], axis=2)
    gate_up_share = lax.all_to_all(gate_up_share, YC, 0, 0, tiled=True).astype(f32)
    ninth = gate_up_share[:, :, PART:].reshape(8, 2048)
    gate_up_share, down_share, *output_delta = tie(gate_up_share, down_share, *output_delta)
    project_delta, output_delta = (sum(p.astype(f32) for p in parts).astype(bf16) for parts in (project_delta, output_delta))
    folded = jnp.pad(project_delta[128:], ((0, 0), (0, 2048 - 1664))).reshape(16, 8, 256)
    mixer_delta = jnp.concatenate(
        [project_delta[:128].reshape(16, 8, 1664), folded, output_delta.reshape(16, 8, D)], axis=2
    )
    mixer_delta = lax.all_to_all(mixer_delta, XZ, 0, 0, tiled=True)
    mixer_delta, *down_parts = tie(mixer_delta, *ring_parts(down_share, X, x_index))
    down_share = sum(part.astype(f32) for part in down_parts)[:OWN]
    mixer_delta = jnp.sum(mixer_delta.astype(f32), axis=0)
    project_delta = jnp.concatenate([mixer_delta[:, :1664], mixer_delta[:, 1664:1920].reshape(1, 2048)[:, :1664]], axis=0)
    query_delta, key_delta, value_delta = project_delta[:, :1024], project_delta[:, 1024:1280], project_delta[:, 1280:1536]
    changes = project_delta[:, 1536:]
    entry_change = gain_change(
        (query_weight, key_weight, value_weight), (query_delta, key_delta, value_delta), entry_gain
    )

    def rows(k):
        share = jnp.concatenate(
            [gate_up_share[:, 8 * k : 8 * k + 8, :PART], ninth[:, None, PART * k : PART * (k + 1)]], axis=1
        )
        return share.reshape(NY, NC, 9, NXH, PART // 2).transpose(2, 0, 3, 1, 4).reshape(9, FF)

    gate_delta, upward_delta = rows(0), rows(1)

    feed_change = gain_change((gate_weight, up_weight), (gate_delta, upward_delta), feed_gain)

    raw_grad = jnp.concatenate([query_raw_grad, key_value_grad.astype(bf16)], axis=1)
    entry_in_grad = dot_nt(raw_grad, project)
    stream_part, _ = norm_back(entry_in_grad, entry_x, inverse_rms(entry_x), entry_scale)
    hidden_delta = middle_grad + split_dot_nt(stream_part, to_mixer)

    return (
        layer_output[None],
        hidden_delta[None],
        entry_change,
        query_delta,
        key_delta,
        value_delta,
        changes[:2, 2],
        changes[:2, 3],
        mixer_delta[:, 1920:],
        changes[:, 0],
        feed_change,
        gate_delta,
        upward_delta,
        down_share,
        changes[:, 1],
    )


def solution(mesh):
    chips = Mesh(mesh.devices.reshape(NY, NXH, NC, NXL, NZ), AXES)
    tokens, row, vector = P(SEQ, CP, None), P(AXES, None), P(AXES)
    return jax.shard_map(
        shards,
        mesh=chips,
        in_specs=(
            tokens, P(SEQ), vector, row, row, row, vector, vector,
            row, vector, vector, row, row, row, vector, tokens,
        ),
        out_specs=(
            tokens, tokens, vector, row, row, row, vector, vector,
            row, vector, vector, row, row, row, vector,
        ),
        check_vma=False,
    )
```
